512 devices in a mesh: tm: 128 (over z, y, x_lo), head: 4 (over x_hi, core).
Axes of the slice: x: 4 (x_hi: 2, x_lo: 2; x = x_hi * 2 + x_lo), y: 4, z: 16, core: 2. Of those that a mesh axis runs over, the one named last changes fastest.
Arguments:
- q_video: bfloat16 [65536, 3072], P('tm', 'head')
- k_video: bfloat16 [65536, 3072], P('tm', 'head')
- v_video: bfloat16 [65536, 3072], P('tm', 'head'), may hold values from -6 to 6
- q_audio: bfloat16 [32768, 3072], P('tm', 'head')
- k_audio: bfloat16 [32768, 3072], P('tm', 'head')
- v_audio: bfloat16 [32768, 3072], P('tm', 'head'), may hold values from -6 to 6
- q_gain_video: float32 [3072], P('head'), may hold values from 0.1 to 1.9
- k_gain_video: float32 [3072], P('head'), may hold values from 0.1 to 1.9
- q_gain_audio: float32 [3072], P('head'), may hold values from 0.1 to 1.9
- k_gain_audio: float32 [3072], P('head'), may hold values from 0.1 to 1.9
- audio_align: int32 [32768], P('tm'), may hold values from 0 to 65535, as said below
- windows: int32 [2, 24], P(None, 'head'), may hold values from 32 to 128
Outputs:
- video_out: bfloat16 [65536, 3072], P('tm', 'head')
- audio_out: bfloat16 [32768, 3072], P('tm', 'head')
The draws below stay inside these ranges and needn't reach their ends.
Inputs may be any that keep to these rules, and one draw needn't show every extreme that they name: audio_align[j] equals 2 j plus an offset of 0 to 48, cut at 65535; it is 0 at j = 0 and 65535 at the last audio token.
All inputs are finite; a program needn't handle non-finite values.
Results may differ from the reference program's by a relative error of at most 0.0096.
Values may be sent and summed in bfloat16 or wider, within the bound.
A program may use at most 64 MiB of HBM per device.

```python
import math
import jax
import jax.numpy as jnp
from jax import lax

HEADS = 24
HEAD_DIM = 128
D = 3072
AUDIO_PER_SLOT = 256
TV_DEV = 512
WINDOW_REACH = 128
WC = 64
DRIFT = 48
TV = 65536
TA = 32768
N_TM = 128


def scaled_base(key, rows, spread):
    col_ramp = 1.0 + (math.sqrt(3.0) - 1.0) * jnp.arange(D, dtype=jnp.float32) / (D - 1)
    col_scale = jnp.exp(jax.random.uniform(jax.random.fold_in(key, 1), (D,), jnp.float32, 0.0, math.log(10.0))) * col_ramp
    row_scale = jnp.exp(jax.random.uniform(jax.random.fold_in(key, 2), (rows, 1), jnp.float32, 0.0, spread))
    return (col_scale, row_scale)


def projected(key, rows, salt):
    key = jax.random.fold_in(key, salt)
    col_scale, row_scale = scaled_base(key, rows, math.log(10.0))
    base = jax.random.normal(jax.random.fold_in(key, 3), (rows, D), jnp.float32)
    whole = base * col_scale * row_scale
    return whole.astype(jnp.bfloat16)


def draw_q_video(key, part):
    return projected(key, TV, 11)


def draw_k_video(key, part):
    return projected(key, TV, 12)


def draw_q_audio(key, part):
    return projected(jax.random.fold_in(key, 500), TA, 13)


def draw_k_audio(key, part):
    return projected(jax.random.fold_in(key, 500), TA, 14)


def draw_audio_align(key, part):
    key = jax.random.fold_in(key, 21)
    offsets = jax.random.randint(jax.random.fold_in(key, 1), (TA,), 0, DRIFT + 1)
    chosen = jax.random.randint(jax.random.fold_in(key, 2), (), 1, TA - 1)
    places = jnp.arange(TA, dtype=jnp.int32)
    offsets = jnp.where(places == chosen, DRIFT, offsets)
    offsets = jnp.where(places == 0, 0, offsets)
    aligned = jnp.minimum(2 * places + offsets, TV - 1)
    aligned = jnp.where(places == TA - 1, TV - 1, aligned)
    return aligned.astype(jnp.int32)


def draw_windows(key, part):
    key = jax.random.fold_in(key, 31)
    widths = jax.random.randint(jax.random.fold_in(key, 1), (2, HEADS), WINDOW_REACH // 4, WINDOW_REACH + 1)
    widest = jax.random.randint(jax.random.fold_in(key, 2), (2, 1), 0, HEADS)
    heads = jnp.arange(HEADS, dtype=jnp.int32)[None, :]
    return jnp.where(heads == widest, WINDOW_REACH, widths).astype(jnp.int32)


def block_scale(stream_key, dims, cuts, least, high):
    level, own = 1.0, jax.random.fold_in(stream_key, 6)
    for axis_at, blocks in cuts:
        draws = jnp.exp(jax.random.uniform(jax.random.fold_in(own, axis_at), (blocks,), jnp.float32, least / len(cuts), high / len(cuts)))
        level = level * jnp.repeat(draws, dims[axis_at] // blocks).reshape([-1 if axis == axis_at else 1 for axis in range(len(dims))])
    return level


def noise(rng, dims, deviation, limit, cuts=(), held_as=jnp.bfloat16):
    entries = deviation * jax.random.normal(rng, dims, jnp.float32)
    if cuts:
        entries = entries * block_scale(rng, dims, cuts, -0.22, 0.18)
    return jnp.clip(entries, -limit, limit).astype(held_as)


def setup_inputs(seed: int = 0) -> dict:
    streams_of = jax.random.split(jax.random.key(seed), 13)
    return {
        "q_video": draw_q_video(jax.random.fold_in(streams_of[12], 71), 0),
        "k_video": draw_k_video(jax.random.fold_in(streams_of[12], 71), 0),
        "v_video": noise(streams_of[2], (TV, D), 1.0, 6.0, ((0, 128), (1, 4))),
        "q_audio": draw_q_audio(jax.random.fold_in(streams_of[12], 71), 0),
        "k_audio": draw_k_audio(jax.random.fold_in(streams_of[12], 71), 0),
        "v_audio": noise(streams_of[5], (TA, D), 1.0, 6.0, ((0, 128), (1, 4))),
        "q_gain_video": jnp.clip(1.0 + 0.18 * jax.random.normal(streams_of[6], (D,), jnp.float32), 0.1, 1.9),
        "k_gain_video": jnp.clip(1.0 + 0.18 * jax.random.normal(streams_of[7], (D,), jnp.float32), 0.1, 1.9),
        "q_gain_audio": jnp.clip(1.0 + 0.18 * jax.random.normal(streams_of[8], (D,), jnp.float32), 0.1, 1.9),
        "k_gain_audio": jnp.clip(1.0 + 0.18 * jax.random.normal(streams_of[9], (D,), jnp.float32), 0.1, 1.9),
        "audio_align": draw_audio_align(jax.random.fold_in(streams_of[12], 71), 0),
        "windows": draw_windows(jax.random.fold_in(streams_of[12], 71), 0),
    }


EPS = 1e-06

def normed(values, gain):
    wide = values.astype(jnp.float32)
    meansq = lax.optimization_barrier(jnp.mean(wide * wide, axis=-1, keepdims=True))
    return (wide * lax.rsqrt(meansq + EPS) * gain).astype(jnp.bfloat16)

def compute_attention(query, keys, values, mask):
    scores = jnp.einsum('rhe,khe->hrk', query.astype(jnp.float32), keys.astype(jnp.float32))
    scores = scores * (1.0 / HEAD_DIM ** 0.5)
    scores = jnp.where(mask, scores, -1e+30)
    top = lax.optimization_barrier(jnp.max(scores, axis=-1, keepdims=True))
    expo = jnp.exp(scores - top)
    probs = (expo / lax.optimization_barrier(jnp.sum(expo, axis=-1, keepdims=True))).astype(jnp.bfloat16)
    return jnp.einsum('hrk,khe->rhe', probs.astype(jnp.float32), values.astype(jnp.float32))

def reference(q_video, k_video, v_video, q_audio, k_audio, v_audio, q_gain_video, k_gain_video, q_gain_audio, k_gain_audio, audio_align, windows):
    qv = normed(q_video, q_gain_video).reshape(TV, HEADS, HEAD_DIM)
    kv = normed(k_video, k_gain_video).reshape(TV, HEADS, HEAD_DIM)
    qa = normed(q_audio, q_gain_audio).reshape(TA, HEADS, HEAD_DIM)
    ka = normed(k_audio, k_gain_audio).reshape(TA, HEADS, HEAD_DIM)
    vv = v_video.reshape(TV, HEADS, HEAD_DIM)
    va = v_audio.reshape(TA, HEADS, HEAD_DIM)
    rim = ((WINDOW_REACH, WINDOW_REACH), (0, 0), (0, 0))
    kvp, vvp, kap, audio_value_padded = (jnp.pad(kv, rim), jnp.pad(vv, rim), jnp.pad(ka, rim), jnp.pad(va, rim))
    alignp = jnp.pad(audio_align, (WINDOW_REACH, WINDOW_REACH))
    wvid = windows[0][:, None, None]
    waud = windows[1][:, None, None]

    def block(blk):
        vstart = (blk * TV_DEV).astype(jnp.int32)
        audio_begin_row = (blk * AUDIO_PER_SLOT).astype(jnp.int32)
        qpos = vstart + jnp.arange(TV_DEV, dtype=jnp.int32)
        kpos = vstart - WINDOW_REACH + jnp.arange(TV_DEV + 2 * WINDOW_REACH, dtype=jnp.int32)
        kval = (kpos >= 0) & (kpos < TV)
        aqpos = audio_begin_row + jnp.arange(AUDIO_PER_SLOT, dtype=jnp.int32)
        apos = audio_begin_row - WINDOW_REACH + jnp.arange(AUDIO_PER_SLOT + 2 * WINDOW_REACH, dtype=jnp.int32)
        aval = (apos >= 0) & (apos < TA)
        video_query_block = lax.dynamic_slice_in_dim(qv, vstart, TV_DEV, 0)
        audio_query_block = lax.dynamic_slice_in_dim(qa, audio_begin_row, AUDIO_PER_SLOT, 0)
        video_key_block = lax.dynamic_slice_in_dim(kvp, vstart, TV_DEV + 2 * WINDOW_REACH, 0)
        video_value_block = lax.dynamic_slice_in_dim(vvp, vstart, TV_DEV + 2 * WINDOW_REACH, 0)
        audio_key_block = lax.dynamic_slice_in_dim(kap, audio_begin_row, AUDIO_PER_SLOT + 2 * WINDOW_REACH, 0)
        audio_value_block = lax.dynamic_slice_in_dim(audio_value_padded, audio_begin_row, AUDIO_PER_SLOT + 2 * WINDOW_REACH, 0)
        align_keys = lax.dynamic_slice_in_dim(alignp, audio_begin_row, AUDIO_PER_SLOT + 2 * WINDOW_REACH, 0)
        align_rows = lax.dynamic_slice_in_dim(audio_align, audio_begin_row, AUDIO_PER_SLOT, 0)
        video_self_output = (jnp.abs(qpos[:, None] - kpos[None, :])[None] <= wvid) & kval[None, None, :]
        video_cross_output = ((jnp.abs(align_keys[None, :] - qpos[:, None]) <= WC) & aval[None, :])[None]
        audio_self_output = (jnp.abs(aqpos[:, None] - apos[None, :])[None] <= waud) & aval[None, None, :]
        audio_cross_output = ((jnp.abs(align_rows[:, None] - kpos[None, :]) <= WC) & kval[None, :])[None]
        video_tokens = compute_attention(video_query_block, video_key_block, video_value_block, video_self_output) + compute_attention(video_query_block, audio_key_block, audio_value_block, video_cross_output)
        audio_tokens = compute_attention(audio_query_block, audio_key_block, audio_value_block, audio_self_output) + compute_attention(audio_query_block, video_key_block, video_value_block, audio_cross_output)
        return (video_tokens.reshape(TV_DEV, D).astype(jnp.bfloat16), audio_tokens.reshape(AUDIO_PER_SLOT, D).astype(jnp.bfloat16))
    vids, auds = lax.map(block, jnp.arange(N_TM, dtype=jnp.int32))
    return (vids.reshape(TV, D), auds.reshape(TA, D))
```

```python
import functools
import math

import jax
import jax.numpy as jnp
from jax import lax
from jax.experimental import pallas as pl
from jax.experimental.pallas import tpu as pltpu
from jax.sharding import PartitionSpec as P

HEAD_DIM = 128
D = 3072
WC = 64
EPS = 1e-06
B = 128
NEG = -1e30
C = math.log2(math.e) / math.sqrt(HEAD_DIM)
MESH = pl.DeviceIdType.MESH
HEADS_AHEAD = 2

ROW_QV, ROW_KV, ROW_QA, ROW_KA, ROW_ALIGN = 0, 4, 8, 10, 12


def dot_nt(a, b):
    return lax.dot_general(a, b, (((1,), (1,)), ((), ())), preferred_element_type=jnp.float32)


def dot_nn(a, b):
    return jnp.dot(a, b, preferred_element_type=jnp.float32)


def with_ones(v):
    return jnp.concatenate([v, jnp.ones(v.shape, v.dtype)], axis=1)


def column(row):
    return jnp.broadcast_to(row, (B, B)).T


def partial_softmax(q, k, v, bias):
    s = dot_nt(q, k) + bias
    m = jnp.max(s, axis=1, keepdims=True)
    p = jnp.exp2((s - m) * C).astype(jnp.bfloat16)
    return m, dot_nn(p, with_ones(v))


def merged(q, k, v, bias, m0, o0):
    s = dot_nt(q, k) + bias
    m1 = jnp.maximum(m0, jnp.max(s, axis=1, keepdims=True))
    p = jnp.exp2((s - m1) * C).astype(jnp.bfloat16)
    a = jnp.exp2((m0 - m1) * C)
    return o0 * jnp.concatenate([a, a], axis=1) + dot_nn(p, with_ones(v))


def ratio(o):
    return o[:, :B] / o[:, B:]


def kernel(
    n_tm, n_head, heads,
    windows, gqv, gkv, gqa, gka, align,
    qv_hbm, kv_hbm, vv_hbm, qa_hbm, ka_hbm, va_hbm,
    ov_hbm, oa_hbm,
    qv, kv, vv, qa, ka, va, halo,
    sums, nb, nbr, fcol, hcol,
    self_bias, va_bias, av_bias, vah_bias, avh_bias,
    qvn, kvn, qan, kan, ms, os, ov, oa,
    load_sem, hsend, hrecv, ssend, srecv, nsend, nrecv, out_sem,
):
    me = lax.axis_index("tm")
    hd = lax.axis_index("head")
    right = lax.rem(me + 1, n_tm)
    left = lax.rem(me + n_tm - 1, n_tm)
    peers = [lax.rem(hd + i, n_head) for i in range(1, n_head)]
    sources = (kv_hbm, vv_hbm, ka_hbm, va_hbm)
    loads = ((qv_hbm, qv), (kv_hbm, kv), (qa_hbm, qa), (ka_hbm, ka), (vv_hbm, vv), (va_hbm, va))

    def columns(h):
        start = h * HEAD_DIM
        return pl.ds(start if isinstance(h, int) else pl.multiple_of(start, HEAD_DIM), HEAD_DIM)

    def load(i, h):
        src, dst = loads[i]
        return pltpu.make_async_copy(src.at[:, columns(h)], dst.at[h], load_sem.at[i, h])

    def halo_copy(h, side, a):
        src = sources[a]
        row = src.shape[0] - B if side == 0 else 0
        return pltpu.make_async_remote_copy(
            src_ref=src.at[pl.ds(row, B), columns(h)],
            dst_ref=halo.at[h, side, a],
            send_sem=hsend.at[h, side, a],
            recv_sem=hrecv.at[h, side, a],
            device_id=(right if side == 0 else left, hd),
            device_id_type=MESH,
        )

    def start_halo(h):
        for a in range(4):
            for side in (0, 1):
                halo_copy(h, side, a).start()

    sums[0] = jnp.zeros((16, B), jnp.float32)
    barrier = pltpu.get_barrier_semaphore()
    for device in [(right, hd), (left, hd)] + [(me, p) for p in peers]:
        pl.semaphore_signal(barrier, inc=1, device_id=device, device_id_type=MESH)
    for i in range(6):
        for h in range(heads):
            load(i, h).start()
    pl.semaphore_wait(barrier, 1 + n_head)
    for h in range(HEADS_AHEAD):
        start_halo(h)

    for i in range(4):
        for h in range(heads):
            load(i, h).wait()
    for ref, row in ((qv, ROW_QV), (kv, ROW_KV), (qa, ROW_QA), (ka, ROW_KA)):
        for r in range(ref.shape[1] // B):
            total = None
            for h in range(heads):
                x = ref[h, r * B : (r + 1) * B, :].astype(jnp.float32)
                total = x * x if total is None else total + x * x
            sums[0, row + r : row + r + 1, :] = jnp.sum(total.T, axis=0, keepdims=True)
    exchange = [
        pltpu.make_async_remote_copy(
            src_ref=sums.at[0],
            dst_ref=sums.at[1 + i],
            send_sem=ssend.at[i],
            recv_sem=srecv.at[i],
            device_id=(me, p),
            device_id_type=MESH,
        )
        for i, p in enumerate(peers)
    ]
    for copy in exchange:
        copy.start()

    v0 = (me * qv.shape[1]).astype(jnp.float32)
    al = align[...].astype(jnp.float32)
    rows = lax.broadcasted_iota(jnp.int32, (B, B), 0)
    cols = lax.broadcasted_iota(jnp.int32, (B, B), 1)
    rowsf = rows.astype(jnp.float32)
    colsf = cols.astype(jnp.float32)

    def near(x, y):
        return jnp.where(jnp.abs(x - y) <= WC, 0.0, NEG).astype(jnp.float32)

    for b in range(4):
        for j in range(2):
            va_bias[b * B : (b + 1) * B, j * B : (j + 1) * B] = near(
                al[j : j + 1, :], rowsf + (v0 + b * B)
            )
    for j in range(2):
        acol = column(al[j : j + 1, :])
        for t in range(3):
            av_bias[j, :, t * B : (t + 1) * B] = near(acol, colsf + (v0 + (j + t) * B))

    for copy in exchange:
        copy.wait()
    total = sums[0]
    for i in range(1, n_head):
        total = total + sums[i]
    nb[...] = lax.rsqrt(total / D + EPS)
    nb[ROW_ALIGN : ROW_ALIGN + 2, :] = al
    to_neighbours = [
        pltpu.make_async_remote_copy(
            src_ref=nb,
            dst_ref=nbr.at[side],
            send_sem=nsend.at[side],
            recv_sem=nrecv.at[side],
            device_id=(right if side == 0 else left, hd),
            device_id_type=MESH,
        )
        for side in (0, 1)
    ]
    for copy in to_neighbours:
        copy.start()
    for c in range(12):
        fcol[c] = column(nb[c : c + 1, :])
    for i in (4, 5):
        for h in range(heads):
            load(i, h).wait()
    no_left = jnp.where(me == 0, NEG, 0.0).astype(jnp.float32)
    no_right = jnp.where(me == n_tm - 1, NEG, 0.0).astype(jnp.float32)
    for copy in to_neighbours:
        copy.wait()
    for side in (0, 1):
        none = no_left if side == 0 else no_right
        rk, ra, rl = ((ROW_KV + 3, ROW_KA + 1, ROW_ALIGN + 1), (ROW_KV, ROW_KA, ROW_ALIGN))[side]
        hcol[side, 0] = column(nbr[side, rk : rk + 1, :])
        hcol[side, 1] = column(nbr[side, ra : ra + 1, :])
        vah_bias[side] = near(nbr[side, rl : rl + 1, :], rowsf + (v0 + 3 * side * B)) + none
        acol = column(al[side : side + 1, :])
        avh_bias[side] = near(acol, colsf + (v0 + (-B if side == 0 else 4 * B))) + none

    def head(h, carry):
        gains = [g[pl.ds(h, 1), :] for g in (gqv, gkv, gqa, gka)]

        def normed(x, factor, gain):
            return (x.astype(jnp.float32) * factor * gain).astype(jnp.bfloat16)

        for src, dst, row, g in (
            (qv, qvn, ROW_QV, 0), (kv, kvn, ROW_KV, 1), (qa, qan, ROW_QA, 2), (ka, kan, ROW_KA, 3),
        ):
            for r in range(src.shape[1] // B):
                part = slice(r * B, (r + 1) * B)
                dst[part, :] = normed(src[h, part, :], fcol[row + r], gains[g])
        for kind in (0, 1):
            w = windows[kind, h]
            for t in range(3):
                far = jnp.abs(cols - rows + (t - 1) * B)
                self_bias[kind, :, t * B : (t + 1) * B] = jnp.where(far <= w, 0.0, NEG).astype(
                    jnp.float32
                )

        def keep(i, m, o):
            ms[i] = jnp.broadcast_to(m, (B, B))
            os[i] = o

        for b in range(4):
            q = qvn[b * B : (b + 1) * B, :]
            lo, hi = max(b - 1, 0), min(b + 2, 4)
            part = slice(lo * B, hi * B)
            bias = self_bias[0, :, (lo - b + 1) * B : (hi - b + 1) * B]
            m_s, o_s = partial_softmax(q, kvn[part, :], vv[h, part, :], bias)
            part = (slice(0, B), slice(0, 2 * B), slice(0, 2 * B), slice(B, 2 * B))[b]
            m_c, o_c = partial_softmax(
                q, kan[part, :], va[h, part, :], va_bias[b * B : (b + 1) * B, part]
            )
            if b in (1, 2):
                ov[h, b * B : (b + 1) * B, :] = (ratio(o_s) + ratio(o_c)).astype(jnp.bfloat16)
            else:
                keep(2 * (b // 3), m_s, o_s)
                keep(2 * (b // 3) + 1, m_c, o_c)
        for j in range(2):
            q = qan[j * B : (j + 1) * B, :]
            bias = self_bias[1, :, (1 - j) * B : (3 - j) * B]
            m_s, o_s = partial_softmax(q, kan[...], va[h], bias)
            part = slice(j * B, (j + 3) * B)
            m_c, o_c = partial_softmax(q, kvn[part, :], vv[h, part, :], av_bias[j])
            keep(4 + 2 * j, m_s, o_s)
            keep(5 + 2 * j, m_c, o_c)

        for a in range(4):
            for side in (0, 1):
                halo_copy(h, side, a).wait()

        @pl.when(h + HEADS_AHEAD < heads)
        def _():
            start_halo(h + HEADS_AHEAD)

        for side in (0, 1):
            none = no_left if side == 0 else no_right
            hk = normed(halo[h, side, 0], hcol[side, 0], gains[1])
            hv = halo[h, side, 1]
            hka = normed(halo[h, side, 2], hcol[side, 1], gains[3])
            hva = halo[h, side, 3]
            b = 3 * side
            part = slice(b * B, (b + 1) * B)
            q = qvn[part, :]
            edge = slice(2 * side * B, (2 * side + 1) * B)
            o_s = merged(q, hk, hv, self_bias[0, :, edge] + none, ms[2 * side], os[2 * side])
            o_c = merged(q, hka, hva, vah_bias[side], ms[2 * side + 1], os[2 * side + 1])
            ov[h, part, :] = (ratio(o_s) + ratio(o_c)).astype(jnp.bfloat16)
            part = slice(side * B, (side + 1) * B)
            q = qan[part, :]
            o_s = merged(q, hka, hva, self_bias[1, :, edge] + none, ms[4 + 2 * side], os[4 + 2 * side])
            o_c = merged(q, hk, hv, avh_bias[side], ms[5 + 2 * side], os[5 + 2 * side])
            oa[h, part, :] = (ratio(o_s) + ratio(o_c)).astype(jnp.bfloat16)
        pltpu.make_async_copy(ov.at[h], ov_hbm.at[:, columns(h)], out_sem.at[0, h]).start()
        pltpu.make_async_copy(oa.at[h], oa_hbm.at[:, columns(h)], out_sem.at[1, h]).start()
        return carry

    lax.fori_loop(0, heads, head, 0)
    for h in range(heads):
        pltpu.make_async_copy(ov.at[h], ov_hbm.at[:, columns(h)], out_sem.at[0, h]).wait()
        pltpu.make_async_copy(oa.at[h], oa_hbm.at[:, columns(h)], out_sem.at[1, h]).wait()


def body(
    q_video, k_video, v_video, q_audio, k_audio, v_audio,
    q_gain_video, k_gain_video, q_gain_audio, k_gain_audio, audio_align, windows,
):
    n_tm, n_head = lax.axis_size("tm"), lax.axis_size("head")
    rows_v, width = q_video.shape
    rows_a = q_audio.shape[0]
    heads = width // HEAD_DIM
    gains = [
        g.reshape(heads, HEAD_DIM) for g in (q_gain_video, k_gain_video, q_gain_audio, k_gain_audio)
    ]
    bf, f32 = jnp.bfloat16, jnp.float32
    vmem = pl.BlockSpec(memory_space=pltpu.VMEM)
    hbm = pl.BlockSpec(memory_space=pltpu.HBM)
    dma = pltpu.SemaphoreType.DMA
    return pl.pallas_call(
        functools.partial(kernel, n_tm, n_head, heads),
        out_shape=(
            jax.ShapeDtypeStruct(q_video.shape, bf),
            jax.ShapeDtypeStruct(q_audio.shape, bf),
        ),
        in_specs=[pl.BlockSpec(memory_space=pltpu.SMEM)] + [vmem] * 5 + [hbm] * 6,
        out_specs=(hbm, hbm),
        scratch_shapes=[
            pltpu.VMEM((heads, rows_v, B), bf),
            pltpu.VMEM((heads, rows_v, B), bf),
            pltpu.VMEM((heads, rows_v, B), bf),
            pltpu.VMEM((heads, rows_a, B), bf),
            pltpu.VMEM((heads, rows_a, B), bf),
            pltpu.VMEM((heads, rows_a, B), bf),
            pltpu.VMEM((heads, 2, 4, B, B), bf),
            pltpu.VMEM((n_head, 16, B), f32),
            pltpu.VMEM((16, B), f32),
            pltpu.VMEM((2, 16, B), f32),
            pltpu.VMEM((12, B, B), f32),
            pltpu.VMEM((2, 2, B, B), f32),
            pltpu.VMEM((2, B, 3 * B), f32),
            pltpu.VMEM((rows_v, rows_a), f32),
            pltpu.VMEM((2, B, 3 * B), f32),
            pltpu.VMEM((2, B, B), f32),
            pltpu.VMEM((2, B, B), f32),
            pltpu.VMEM((rows_v, B), bf),
            pltpu.VMEM((rows_v, B), bf),
            pltpu.VMEM((rows_a, B), bf),
            pltpu.VMEM((rows_a, B), bf),
            pltpu.VMEM((8, B, B), f32),
            pltpu.VMEM((8, B, 2 * B), f32),
            pltpu.VMEM((heads, rows_v, B), bf),
            pltpu.VMEM((heads, rows_a, B), bf),
            dma((6, heads)),
            dma((heads, 2, 4)),
            dma((heads, 2, 4)),
            dma((n_head - 1,)),
            dma((n_head - 1,)),
            dma((2,)),
            dma((2,)),
            dma((2, heads)),
        ],
        compiler_params=pltpu.CompilerParams(
            collective_id=0, has_side_effects=True, vmem_limit_bytes=60 * 2**20
        ),
        name="attention",
    )(
        windows, *gains, audio_align.reshape(rows_a // B, B),
        q_video, k_video, v_video, q_audio, k_audio, v_audio,
    )


def solution(mesh):
    placed = (P("tm", "head"),) * 6 + (P("head"),) * 4 + (P("tm"), P(None, "head"))
    return jax.shard_map(
        body,
        mesh=mesh,
        in_specs=placed,
        out_specs=(P("tm", "head"), P("tm", "head")),
        check_vma=False,
    )
```

```python
import functools
import math

import jax
import jax.numpy as jnp
from jax import lax
from jax.experimental import pallas as pl
from jax.experimental.pallas import tpu as pltpu
from jax.sharding import PartitionSpec as P

HEAD_DIM = 128
D = 3072
WC = 64
EPS = 1e-06
B = 128
NEG = -1e30
C = math.log2(math.e) / math.sqrt(HEAD_DIM)
MESH = pl.DeviceIdType.MESH

ROW_QV, ROW_KV, ROW_QA, ROW_KA, ROW_ALIGN = 0, 4, 8, 10, 12

VIDEO_SELF = ((0, 256), (0, 384), (128, 512), (256, 512))
VIDEO_CROSS = ((0, 96), (0, 160), (64, 224), (128, 256))
AUDIO_SELF = ((0, 256), (0, 256))
AUDIO_CROSS = ((0, 368), (192, 512))
HALO_VIDEO_CROSS = ((64, 128), (0, 32))
HALO_AUDIO_CROSS = ((64, 128), (0, 112))


def dot_nt(a, b):
    return lax.dot_general(a, b, (((1,), (1,)), ((), ())), preferred_element_type=jnp.float32)


def dot_nn(a, b):
    return jnp.dot(a, b, preferred_element_type=jnp.float32)


def column(row):
    return jnp.broadcast_to(row, (B, B)).T


def softened(s):
    m = jnp.max(s, axis=0, keepdims=True)
    e = jnp.exp2((s - m) * C)
    return m, jnp.sum(e, axis=0, keepdims=True), e.astype(jnp.bfloat16)


def padded(p, first, rows):
    last = rows - first - p.shape[0]
    parts = [jnp.zeros((first, B), p.dtype)] if first else []
    parts.append(p)
    if last:
        parts.append(jnp.zeros((last, B), p.dtype))
    return jnp.concatenate(parts, axis=0) if len(parts) > 1 else p


def in_turn(tasks):
    n = len(tasks)
    tasks[0][0]()
    for i in range(n):
        if i + 1 < n:
            tasks[i + 1][0]()
        tasks[i][1]()
        if i > 0:
            tasks[i - 1][2]()
    tasks[n - 1][2]()


def kernel(
    n_tm, n_head, heads,
    windows, gqv, gkv, gqa, gka, align,
    qv_hbm, kv_hbm, vv_hbm, qa_hbm, ka_hbm, va_hbm,
    ov, oa,
    qv, kv, vv, qa, ka, va, halo,
    sums, nb, nbr, fcol, hcol,
    self_bias, va_bias, av_bias, vah_bias, avh_bias,
    qvn, kvn, qan, kan, vvt, vat, qe, ml, os,
    load_sem, hsend, hrecv, ssend, srecv, nsend, nrecv,
):
    me = lax.axis_index("tm")
    hd = lax.axis_index("head")
    right = jnp.minimum(me + 1, n_tm - 1)
    left = jnp.maximum(me - 1, 0)
    has_left = me > 0
    has_right = me < n_tm - 1
    sends_to = (has_right, has_left)
    comes_from = (has_left, has_right)
    peers = [lax.rem(hd + i, n_head) for i in range(1, n_head)]
    sources = (kv_hbm, vv_hbm, ka_hbm, va_hbm)
    loads = ((qv_hbm, qv), (kv_hbm, kv), (qa_hbm, qa), (ka_hbm, ka), (vv_hbm, vv), (va_hbm, va))

    def columns(h):
        start = h * HEAD_DIM
        return pl.ds(start if isinstance(h, int) else pl.multiple_of(start, HEAD_DIM), HEAD_DIM)

    def load(i, h):
        src, dst = loads[i]
        return pltpu.make_async_copy(src.at[:, columns(h)], dst.at[h], load_sem.at[i, h])

    def halo_copy(h, side, a):
        src = sources[a]
        row = src.shape[0] - B if side == 0 else 0
        return pltpu.make_async_remote_copy(
            src_ref=src.at[pl.ds(row, B), columns(h)],
            dst_ref=halo.at[h, side, a],
            send_sem=hsend.at[h, side, a],
            recv_sem=hrecv.at[h, side, a],
            device_id=(right if side == 0 else left, hd),
            device_id_type=MESH,
        )

    def start_halo(h):
        for side in (0, 1):

            @pl.when(sends_to[side])
            def _():
                for a in range(4):
                    halo_copy(h, side, a).start()

    def wait_halo(h):
        for side in (0, 1):

            @pl.when(comes_from[side])
            def _():
                for a in range(4):
                    halo_copy(h, side, a).wait_recv()

    sums[0] = jnp.zeros((16, B), jnp.float32)
    barrier = pltpu.get_barrier_semaphore()
    for p in peers:
        pl.semaphore_signal(barrier, inc=1, device_id=(me, p), device_id_type=MESH)
    for there, device in ((has_right, right), (has_left, left)):

        @pl.when(there)
        def _():
            pl.semaphore_signal(barrier, inc=1, device_id=(device, hd), device_id_type=MESH)

    for i in range(6):
        for h in range(heads):
            load(i, h).start()
    for slot in (0, 1):

        @pl.when(jnp.logical_not(comes_from[slot]))
        def _():
            nbr[slot] = jnp.zeros((16, B), jnp.float32)

            def clear(h, carry):
                halo[h, slot] = jnp.zeros((4, B, B), jnp.bfloat16)
                return carry

            lax.fori_loop(0, heads, clear, 0)

    pl.semaphore_wait(
        barrier, n_head - 1 + has_left.astype(jnp.int32) + has_right.astype(jnp.int32)
    )
    start_halo(0)

    for i in range(4):
        for h in range(heads):
            load(i, h).wait()
    for ref, row in ((qv, ROW_QV), (kv, ROW_KV), (qa, ROW_QA), (ka, ROW_KA)):
        for r in range(ref.shape[1] // B):
            total = None
            for h in range(heads):
                x = ref[h, r * B : (r + 1) * B, :].astype(jnp.float32)
                total = x * x if total is None else total + x * x
            sums[0, row + r : row + r + 1, :] = jnp.sum(total.T, axis=0, keepdims=True)
    exchange = [
        pltpu.make_async_remote_copy(
            src_ref=sums.at[0],
            dst_ref=sums.at[1 + i],
            send_sem=ssend.at[i],
            recv_sem=srecv.at[i],
            device_id=(me, p),
            device_id_type=MESH,
        )
        for i, p in enumerate(peers)
    ]
    for copy in exchange:
        copy.start()
    start_halo(1)
    start_halo(2)

    v0 = (me * qv.shape[1]).astype(jnp.float32)
    al = align[...].astype(jnp.float32)
    rows = lax.broadcasted_iota(jnp.int32, (B, B), 0)
    cols = lax.broadcasted_iota(jnp.int32, (B, B), 1)
    rowsf = rows.astype(jnp.float32)
    colsf = cols.astype(jnp.float32)

    def near(x, y):
        return jnp.where(jnp.abs(x - y) <= WC, 0.0, NEG).astype(jnp.float32)

    acols = [column(al[j : j + 1, :]) for j in range(2)]
    for b, (lo, hi) in enumerate(VIDEO_CROSS):
        for t in range(lo // B, -(-hi // B)):
            first, last = max(lo, t * B), min(hi, (t + 1) * B)
            bias = near(acols[t], colsf + (v0 + b * B))
            va_bias[b, first - lo : last - lo, :] = bias[first - t * B : last - t * B, :]
    for j, (lo, hi) in enumerate(AUDIO_CROSS):
        for t in range(lo // B, -(-hi // B)):
            first, last = max(lo, t * B), min(hi, (t + 1) * B)
            bias = near(al[j : j + 1, :], rowsf + (v0 + t * B))
            av_bias[j, first - lo : last - lo, :] = bias[first - t * B : last - t * B, :]

    for i in (4, 5):
        for h in range(heads):
            load(i, h).wait()

    def turn_values(h, carry):
        for src, dst in ((vv, vvt), (va, vat)):
            for r in range(src.shape[1] // B):
                dst[h, :, r * B : (r + 1) * B] = src[h, r * B : (r + 1) * B, :].T
        return carry

    lax.fori_loop(0, heads, turn_values, 0)

    for copy in exchange:
        copy.wait()
    total = sums[0]
    for i in range(1, n_head):
        total = total + sums[i]
    nb[...] = lax.rsqrt(total / D + EPS)
    nb[ROW_ALIGN : ROW_ALIGN + 2, :] = al
    to_neighbours = [
        pltpu.make_async_remote_copy(
            src_ref=nb,
            dst_ref=nbr.at[side],
            send_sem=nsend.at[side],
            recv_sem=nrecv.at[side],
            device_id=(right if side == 0 else left, hd),
            device_id_type=MESH,
        )
        for side in (0, 1)
    ]
    for side in (0, 1):
        pl.when(sends_to[side])(to_neighbours[side].start)
    for h in range(3, heads):
        start_halo(h)
    for c in range(12):
        fcol[c] = column(nb[c : c + 1, :])
    def normed(x, factor, gain):
        return (x.astype(jnp.float32) * factor * gain).astype(jnp.bfloat16)

    def own_keys(h, carry):
        gains = [g[pl.ds(h, 1), :] for g in (gqv, gkv, gqa, gka)]

        for src, dst, row, g in (
            (qv, qvn, ROW_QV, 0), (kv, kvn, ROW_KV, 1), (qa, qan, ROW_QA, 2), (ka, kan, ROW_KA, 3),
        ):
            for r in range(src.shape[1] // B):
                part = slice(r * B, (r + 1) * B)
                dst[part, :] = normed(src[h, part, :], fcol[row + r], gains[g])
        for kind in (0, 1):
            w = windows[kind, h]
            for t in range(3):
                far = jnp.abs(rows - cols + (t - 1) * B)
                self_bias[h, kind, t * B : (t + 1) * B, :] = jnp.where(far <= w, 0.0, NEG).astype(
                    jnp.float32
                )

        def keep(side, kind, half, m, l, o):
            lanes = slice(half * B, (half + 1) * B)
            row = 4 * side + 2 * kind
            ml[h, row : row + 1, lanes] = m
            ml[h, row + 1 : row + 2, lanes] = l
            os[h, side, kind, :, lanes] = o

        def task(queries, keys, values, windows_of, bias_of, finish):
            lo = min(w[0] for w in windows_of)
            hi = max(w[1] for w in windows_of)
            held = {}

            def scores():
                s = dot_nt(keys[lo:hi, :], queries)
                held["s"] = [
                    s[first - lo : last - lo, i * B : (i + 1) * B]
                    for i, (first, last) in enumerate(windows_of)
                ]

            def weights():
                held["p"] = [softened(held["s"][i] + bias_of(i)) for i in (0, 1)]

            def products():
                p = [
                    padded(held["p"][i][2], windows_of[i][0] - lo, hi - lo) for i in (0, 1)
                ]
                o = dot_nn(values[h, :, lo:hi], jnp.concatenate(p, axis=1))
                finish([(*held["p"][i][:2], o[:, i * B : (i + 1) * B]) for i in (0, 1)])

            return scores, weights, products

        done = {}

        def video_done(pair, kind, results):
            done[pair, kind] = results
            if (pair, 1 - kind) not in done:
                return
            for i in (0, 1):
                b = 2 * pair + i
                if b in (1, 2):
                    o = sum(done[pair, k][i][2] * (1.0 / done[pair, k][i][1]) for k in (0, 1))
                    ov[b * B : (b + 1) * B, columns(h)] = o.astype(jnp.bfloat16).T
                else:
                    for k in (0, 1):
                        keep(pair, k, 0, *done[pair, k][i])

        def audio_done(kind, results):
            for side in (0, 1):
                keep(side, kind, 1, *results[side])

        tasks = []
        for pair in (0, 1):
            q = qvn[2 * pair * B : 2 * (pair + 1) * B, :]
            part = VIDEO_SELF[2 * pair : 2 * pair + 2]

            def self_of(i, pair=pair):
                lo, hi = VIDEO_SELF[2 * pair + i]
                shift = (1 - 2 * pair - i) * B
                return self_bias[h, 0, lo + shift : hi + shift, :]

            tasks.append(
                task(q, kvn, vvt, part, self_of, functools.partial(video_done, pair, 0))
            )
            part = VIDEO_CROSS[2 * pair : 2 * pair + 2]

            def cross_of(i, pair=pair):
                lo, hi = VIDEO_CROSS[2 * pair + i]
                return va_bias[2 * pair + i, 0 : hi - lo, :]

            tasks.append(
                task(q, kan, vat, part, cross_of, functools.partial(video_done, pair, 1))
            )
        tasks.append(
            task(
                qan[...], kvn, vvt, AUDIO_CROSS,
                lambda j: av_bias[j, 0 : AUDIO_CROSS[j][1] - AUDIO_CROSS[j][0], :],
                functools.partial(audio_done, 0),
            )
        )
        tasks.append(
            task(
                qan[...], kan, vat, AUDIO_SELF,
                lambda j: self_bias[h, 1, (1 - j) * B : (3 - j) * B, :],
                functools.partial(audio_done, 1),
            )
        )
        in_turn(tasks)
        for side in (0, 1):
            qe[h, side, :B, :] = qvn[3 * side * B : (3 * side + 1) * B, :]
            qe[h, side, B:, :] = qan[side * B : (side + 1) * B, :]
        return carry

    lax.fori_loop(0, heads, own_keys, 0)

    no_left = jnp.where(me == 0, NEG, 0.0).astype(jnp.float32)
    no_right = jnp.where(me == n_tm - 1, NEG, 0.0).astype(jnp.float32)
    for side in (0, 1):
        pl.when(comes_from[side])(to_neighbours[side].wait_recv)
    for side in (0, 1):
        none = no_left if side == 0 else no_right
        rk, ra, rl = ((ROW_KV + 3, ROW_KA + 1, ROW_ALIGN + 1), (ROW_KV, ROW_KA, ROW_ALIGN))[side]
        hcol[side, 0] = column(nbr[side, rk : rk + 1, :])
        hcol[side, 1] = column(nbr[side, ra : ra + 1, :])
        acol = column(nbr[side, rl : rl + 1, :])
        vah_bias[side] = near(acol, colsf + (v0 + 3 * side * B)) + none
        avh_bias[side] = near(al[side : side + 1, :], rowsf + (v0 + (-B if side == 0 else 4 * B))) + none

    def neighbour_keys(h, carry):
        gains = [g[pl.ds(h, 1), :] for g in (gkv, gka)]
        wait_halo(h)
        total = {}

        def task(side, kind):
            none = no_left if side == 0 else no_right
            edge = slice(2 * side * B, (2 * side + 1) * B)
            reach = (HALO_AUDIO_CROSS, HALO_VIDEO_CROSS)[kind][side]
            cross = (avh_bias, vah_bias)[kind]
            row = 4 * side + 2 * kind
            held = {}

            def scores():
                keys = normed(halo[h, side, 2 * kind], hcol[side, kind], gains[kind])
                held["s"] = dot_nt(keys, qe[h, side])

            def weights():
                results = []
                for i in (0, 1):
                    lanes = slice(i * B, (i + 1) * B)
                    first, last = (0, B) if i == kind else reach
                    if i == kind:
                        bias = self_bias[h, kind, edge, :] + none
                    else:
                        bias = cross[side, first:last, :]
                    s = held["s"][first:last, lanes] + bias
                    m0 = ml[h, row : row + 1, lanes]
                    m = jnp.maximum(m0, jnp.max(s, axis=0, keepdims=True))
                    e = jnp.exp2((s - m) * C)
                    a = jnp.exp2((m0 - m) * C)
                    l = ml[h, row + 1 : row + 2, lanes] * a + jnp.sum(e, axis=0, keepdims=True)
                    results.append((a, l, padded(e.astype(jnp.bfloat16), first, B)))
                held["p"] = results

            def products():
                values = halo[h, side, 2 * kind + 1].T
                o = dot_nn(values, jnp.concatenate([p[2] for p in held["p"]], axis=1))
                for i in (0, 1):
                    lanes = slice(i * B, (i + 1) * B)
                    a, l, _ = held["p"][i]
                    total[kind, i] = (os[h, side, kind, :, lanes] * a + o[:, lanes]) * (1.0 / l)
                if kind == 1:
                    part = slice(3 * side * B, (3 * side + 1) * B)
                    o = total[0, 0] + total[1, 0]
                    ov[part, columns(h)] = o.astype(jnp.bfloat16).T
                    part = slice(side * B, (side + 1) * B)
                    o = total[0, 1] + total[1, 1]
                    oa[part, columns(h)] = o.astype(jnp.bfloat16).T

            return scores, weights, products

        in_turn([task(side, kind) for side in (0, 1) for kind in (0, 1)])
        return carry

    lax.fori_loop(0, heads, neighbour_keys, 0)
    for side in (0, 1):

        @pl.when(sends_to[side])
        def _():
            to_neighbours[side].wait_send()

            def sent(h, carry):
                for a in range(4):
                    halo_copy(h, side, a).wait_send()
                return carry

            lax.fori_loop(0, heads, sent, 0)


def body(
    q_video, k_video, v_video, q_audio, k_audio, v_audio,
    q_gain_video, k_gain_video, q_gain_audio, k_gain_audio, audio_align, windows,
):
    n_tm, n_head = lax.axis_size("tm"), lax.axis_size("head")
    rows_v, width = q_video.shape
    rows_a = q_audio.shape[0]
    heads = width // HEAD_DIM
    gains = [
        g.reshape(heads, HEAD_DIM) for g in (q_gain_video, k_gain_video, q_gain_audio, k_gain_audio)
    ]
    bf, f32 = jnp.bfloat16, jnp.float32
    vmem = pl.BlockSpec(memory_space=pltpu.VMEM)
    hbm = pl.BlockSpec(memory_space=pltpu.HBM)
    dma = pltpu.SemaphoreType.DMA
    return pl.pallas_call(
        functools.partial(kernel, n_tm, n_head, heads),
        out_shape=(
            pltpu.VMEM(q_video.shape, bf),
            pltpu.VMEM(q_audio.shape, bf),
        ),
        in_specs=[pl.BlockSpec(memory_space=pltpu.SMEM)] + [vmem] * 5 + [hbm] * 6,
        out_specs=(vmem, vmem),
        scratch_shapes=[
            pltpu.VMEM((heads, rows_v, B), bf),
            pltpu.VMEM((heads, rows_v, B), bf),
            pltpu.VMEM((heads, rows_v, B), bf),
            pltpu.VMEM((heads, rows_a, B), bf),
            pltpu.VMEM((heads, rows_a, B), bf),
            pltpu.VMEM((heads, rows_a, B), bf),
            pltpu.VMEM((heads, 2, 4, B, B), bf),
            pltpu.VMEM((n_head, 16, B), f32),
            pltpu.VMEM((16, B), f32),
            pltpu.VMEM((2, 16, B), f32),
            pltpu.VMEM((12, B, B), f32),
            pltpu.VMEM((2, 2, B, B), f32),
            pltpu.VMEM((heads, 2, 3 * B, B), f32),
            pltpu.VMEM((4, 160, B), f32),
            pltpu.VMEM((2, 368, B), f32),
            pltpu.VMEM((2, B, B), f32),
            pltpu.VMEM((2, B, B), f32),
            pltpu.VMEM((rows_v, B), bf),
            pltpu.VMEM((rows_v, B), bf),
            pltpu.VMEM((rows_a, B), bf),
            pltpu.VMEM((rows_a, B), bf),
            pltpu.VMEM((heads, B, rows_v), bf),
            pltpu.VMEM((heads, B, rows_a), bf),
            pltpu.VMEM((heads, 2, 2 * B, B), bf),
            pltpu.VMEM((heads, 8, 2 * B), f32),
            pltpu.VMEM((heads, 2, 2, B, 2 * B), f32),
            dma((6, heads)),
            dma((heads, 2, 4)),
            dma((heads, 2, 4)),
            dma((n_head - 1,)),
            dma((n_head - 1,)),
            dma((2,)),
            dma((2,)),
        ],
        compiler_params=pltpu.CompilerParams(
            collective_id=0, has_side_effects=True, vmem_limit_bytes=60 * 2**20
        ),
        name="attention",
    )(
        windows, *gains, audio_align.reshape(rows_a // B, B),
        q_video, k_video, v_video, q_audio, k_audio, v_audio,
    )


def solution(mesh):
    placed = (P("tm", "head"),) * 6 + (P("head"),) * 4 + (P("tm"), P(None, "head"))
    return jax.shard_map(
        body,
        mesh=mesh,
        in_specs=placed,
        out_specs=(P("tm", "head"), P("tm", "head")),
        check_vma=False,
    )
```

```python
import functools
import math

import jax
import jax.numpy as jnp
from jax import lax
from jax.experimental import pallas as pl
from jax.experimental.pallas import tpu as pltpu
from jax.sharding import PartitionSpec as P

HEAD_DIM = 128
D = 3072
WC = 64
EPS = 1e-06
B = 128
NEG = -1e30
C = math.log2(math.e) / math.sqrt(HEAD_DIM)
MESH = pl.DeviceIdType.MESH

ROW_QV, ROW_KV, ROW_QA, ROW_KA = 0, 4, 8, 10

VIDEO_SELF = ((0, 256), (0, 384), (128, 512), (256, 512))
VIDEO_CROSS = ((0, 96), (0, 160), (64, 224), (128, 256))
AUDIO_SELF = ((0, 256), (0, 256))
AUDIO_CROSS = ((0, 368), (192, 512))
HALO_VIDEO_CROSS = ((64, 128), (0, 32))
HALO_AUDIO_CROSS = ((64, 128), (0, 112))


def dot_nt(a, b):
    return lax.dot_general(a, b, (((1,), (1,)), ((), ())), preferred_element_type=jnp.float32)


def dot_nn(a, b):
    return jnp.dot(a, b, preferred_element_type=jnp.float32)


def column(row):
    return jnp.broadcast_to(row, (B, B)).T


def softened(s):
    m = jnp.max(s, axis=0, keepdims=True)
    e = jnp.exp2((s - m) * C)
    return m, jnp.sum(e, axis=0, keepdims=True), e.astype(jnp.bfloat16)


def padded(p, first, rows):
    last = rows - first - p.shape[0]
    parts = [jnp.zeros((first, B), p.dtype)] if first else []
    parts.append(p)
    if last:
        parts.append(jnp.zeros((last, B), p.dtype))
    return jnp.concatenate(parts, axis=0) if len(parts) > 1 else p


def in_turn(tasks):
    n = len(tasks)
    tasks[0][0]()
    for i in range(n):
        if i + 1 < n:
            tasks[i + 1][0]()
        tasks[i][1]()
        if i > 0:
            tasks[i - 1][2]()
    tasks[n - 1][2]()


def kernel(
    n_tm, heads,
    windows, gqv_hbm, gkv_hbm, gqa_hbm, gka_hbm, align_hbm,
    qv_hbm, kv_hbm, vv_hbm, qa_hbm, ka_hbm, va_hbm,
    ov, oa,
    gqv, gkv, gqa, gka, align, qv, kv, vv, qa, ka, va, halo,
    sums, nb, nbr, fcol, hcol,
    self_bias, va_bias, av_bias, vah_bias, avh_bias,
    qvn, kvn, qan, kan, vvt, vat, qe, ml, os,
    small_sem, load_sem, hsend, hrecv, ssend, srecv, nsend, nrecv,
):
    me = lax.axis_index("tm")
    hd = lax.axis_index("head")
    right = jnp.minimum(me + 1, n_tm - 1)
    left = jnp.maximum(me - 1, 0)
    has_left = me > 0
    has_right = me < n_tm - 1
    sends_to = (has_right, has_left)
    comes_from = (has_left, has_right)
    peers = [lax.bitwise_xor(hd, 1), lax.bitwise_xor(hd, 2)]
    sources = (kv_hbm, vv_hbm, ka_hbm, va_hbm)
    loads = ((qv_hbm, qv), (kv_hbm, kv), (qa_hbm, qa), (ka_hbm, ka), (vv_hbm, vv), (va_hbm, va))

    def columns(h):
        start = h * HEAD_DIM
        return pl.ds(start if isinstance(h, int) else pl.multiple_of(start, HEAD_DIM), HEAD_DIM)

    def load(i, h):
        src, dst = loads[i]
        return pltpu.make_async_copy(src.at[:, columns(h)], dst.at[h], load_sem.at[i, h])

    small = [
        pltpu.make_async_copy(src, dst, small_sem.at[i])
        for i, (src, dst) in enumerate(
            ((align_hbm, align), (gqv_hbm, gqv), (gkv_hbm, gkv), (gqa_hbm, gqa), (gka_hbm, gka))
        )
    ]

    def halo_copy(h, side, a):
        src = sources[a]
        row = src.shape[0] - B if side == 0 else 0
        return pltpu.make_async_remote_copy(
            src_ref=src.at[pl.ds(row, B), columns(h)],
            dst_ref=halo.at[h, side, a],
            send_sem=hsend.at[h, side, a],
            recv_sem=hrecv.at[h, side, a],
            device_id=(right if side == 0 else left, hd),
            device_id_type=MESH,
        )

    def start_halo(h, kinds=(0, 1)):
        for kind in kinds:
            for side in (0, 1):

                @pl.when(sends_to[side])
                def _():
                    for a in (2 * kind, 2 * kind + 1):
                        halo_copy(h, side, a).start()

    def wait_halo(h, kind):
        for side in (0, 1):

            @pl.when(sends_to[side])
            def _():
                for a in (2 * kind, 2 * kind + 1):
                    halo_copy(h, side, a).wait_send()

        for side in (0, 1):

            @pl.when(comes_from[side])
            def _():
                for a in (2 * kind, 2 * kind + 1):
                    halo_copy(h, side, a).wait_recv()

    sums[0] = jnp.zeros((16, B), jnp.float32)
    nb[...] = jnp.zeros_like(nb)
    barrier = pltpu.get_barrier_semaphore()
    for p in peers:
        pl.semaphore_signal(barrier, inc=1, device_id=(me, p), device_id_type=MESH)
    for there, device in ((has_right, right), (has_left, left)):

        @pl.when(there)
        def _():
            pl.semaphore_signal(barrier, inc=1, device_id=(device, hd), device_id_type=MESH)

    for i in range(4):
        for h in range(heads):
            load(i, h).start()
    for copy in small:
        copy.start()
    for i in (4, 5):
        for h in range(heads):
            load(i, h).start()
    for slot in (0, 1):

        @pl.when(jnp.logical_not(comes_from[slot]))
        def _():
            nbr[slot] = jnp.zeros((8, B), jnp.float32)

            def clear(h, carry):
                halo[h, slot] = jnp.zeros((4, B, B), jnp.bfloat16)
                return carry

            lax.fori_loop(0, heads, clear, 0)

    pl.semaphore_wait(
        barrier, 2 + has_left.astype(jnp.int32) + has_right.astype(jnp.int32)
    )
    start_halo(0, (0,))

    for i in range(4):
        for h in range(heads):
            load(i, h).wait()
    for ref, row in ((qv, ROW_QV), (kv, ROW_KV), (qa, ROW_QA), (ka, ROW_KA)):
        for r in range(ref.shape[1] // B):
            total = None
            for h in range(heads):
                x = ref[h, r * B : (r + 1) * B, :].astype(jnp.float32)
                total = x * x if total is None else total + x * x
            sums[0, row + r : row + r + 1, :] = jnp.sum(total.T, axis=0, keepdims=True)
    exchange = [
        pltpu.make_async_remote_copy(
            src_ref=sums.at[2 * i],
            dst_ref=sums.at[2 * i + 1],
            send_sem=ssend.at[i],
            recv_sem=srecv.at[i],
            device_id=(me, p),
            device_id_type=MESH,
        )
        for i, p in enumerate(peers)
    ]
    exchange[0].start()
    start_halo(0, (1,))

    for copy in small:
        copy.wait()
    v0 = (me * qv.shape[1]).astype(jnp.float32)
    al = align[...].astype(jnp.float32)
    rows = lax.broadcasted_iota(jnp.int32, (B, B), 0)
    cols = lax.broadcasted_iota(jnp.int32, (B, B), 1)
    rowsf = rows.astype(jnp.float32)
    colsf = cols.astype(jnp.float32)

    def near(x, y):
        return jnp.where(jnp.abs(x - y) <= WC, 0.0, NEG).astype(jnp.float32)

    acols = [column(al[j : j + 1, :]) for j in range(2)]
    for b, (lo, hi) in enumerate(VIDEO_CROSS):
        for t in range(lo // B, -(-hi // B)):
            first, last = max(lo, t * B), min(hi, (t + 1) * B)
            bias = near(acols[t], colsf + (v0 + b * B))
            va_bias[b, first - lo : last - lo, :] = bias[first - t * B : last - t * B, :]
    for j, (lo, hi) in enumerate(AUDIO_CROSS):
        for t in range(lo // B, -(-hi // B)):
            first, last = max(lo, t * B), min(hi, (t + 1) * B)
            bias = near(al[j : j + 1, :], rowsf + (v0 + t * B))
            av_bias[j, first - lo : last - lo, :] = bias[first - t * B : last - t * B, :]

    for i in (4, 5):
        for h in range(heads):
            load(i, h).wait()

    exchange[0].wait()
    sums[2] = sums[0] + sums[1]
    exchange[1].start()
    start_halo(1)
    start_halo(2)

    def turn_values(h, carry):
        for src, dst in ((vv, vvt), (va, vat)):
            for r in range(src.shape[1] // B):
                dst[h, :, r * B : (r + 1) * B] = src[h, r * B : (r + 1) * B, :].T
        return carry

    lax.fori_loop(0, heads, turn_values, 0)

    exchange[1].wait()
    factors = lax.rsqrt((sums[2] + sums[3]) / D + EPS)
    for side, picked in enumerate(((ROW_KV + 3, ROW_KA + 1, 1), (ROW_KV, ROW_KA, 0))):
        for i, row in enumerate(picked):
            source = factors if i < 2 else al
            nb[side, i : i + 1, :] = source[row : row + 1, :]
    to_neighbours = [
        pltpu.make_async_remote_copy(
            src_ref=nb.at[side],
            dst_ref=nbr.at[side],
            send_sem=nsend.at[side],
            recv_sem=nrecv.at[side],
            device_id=(right if side == 0 else left, hd),
            device_id_type=MESH,
        )
        for side in (0, 1)
    ]
    for side in (0, 1):
        pl.when(sends_to[side])(to_neighbours[side].start)
    for h in range(3, heads):
        start_halo(h)
    for c in range(12):
        fcol[c] = column(factors[c : c + 1, :])

    def normed(x, factor, gain):
        return (x.astype(jnp.float32) * factor * gain).astype(jnp.bfloat16)

    def own_keys(h, carry):
        gains = [g[pl.ds(h, 1), :] for g in (gqv, gkv, gqa, gka)]

        for src, dst, row, g in (
            (qv, qvn, ROW_QV, 0), (kv, kvn, ROW_KV, 1), (qa, qan, ROW_QA, 2), (ka, kan, ROW_KA, 3),
        ):
            for r in range(src.shape[1] // B):
                part = slice(r * B, (r + 1) * B)
                dst[part, :] = normed(src[h, part, :], fcol[row + r], gains[g])
        for kind in (0, 1):
            w = windows[kind, h]
            for t in range(3):
                far = jnp.abs(rows - cols + (t - 1) * B)
                self_bias[h, kind, t * B : (t + 1) * B, :] = jnp.where(far <= w, 0.0, NEG).astype(
                    jnp.float32
                )

        def keep(side, kind, half, m, l, o):
            lanes = slice(half * B, (half + 1) * B)
            row = 4 * side + 2 * kind
            ml[h, row : row + 1, lanes] = m
            ml[h, row + 1 : row + 2, lanes] = l
            os[h, side, kind, :, lanes] = o

        def task(queries, keys, values, windows_of, bias_of, finish):
            lo = min(w[0] for w in windows_of)
            hi = max(w[1] for w in windows_of)
            held = {}

            def scores():
                s = dot_nt(keys[lo:hi, :], queries)
                held["s"] = [
                    s[first - lo : last - lo, i * B : (i + 1) * B]
                    for i, (first, last) in enumerate(windows_of)
                ]

            def weights():
                held["p"] = [softened(held["s"][i] + bias_of(i)) for i in (0, 1)]

            def products():
                p = [
                    padded(held["p"][i][2], windows_of[i][0] - lo, hi - lo) for i in (0, 1)
                ]
                o = dot_nn(values[h, :, lo:hi], jnp.concatenate(p, axis=1))
                finish([(*held["p"][i][:2], o[:, i * B : (i + 1) * B]) for i in (0, 1)])

            return scores, weights, products

        done = {}

        def video_done(pair, kind, results):
            done[pair, kind] = results
            if (pair, 1 - kind) not in done:
                return
            for i in (0, 1):
                b = 2 * pair + i
                if b in (1, 2):
                    o = sum(done[pair, k][i][2] * (1.0 / done[pair, k][i][1]) for k in (0, 1))
                    ov[b * B : (b + 1) * B, columns(h)] = o.astype(jnp.bfloat16).T
                else:
                    for k in (0, 1):
                        keep(pair, k, 0, *done[pair, k][i])

        def audio_done(kind, results):
            for side in (0, 1):
                keep(side, kind, 1, *results[side])

        tasks = []
        for pair in (0, 1):
            q = qvn[2 * pair * B : 2 * (pair + 1) * B, :]
            part = VIDEO_SELF[2 * pair : 2 * pair + 2]

            def self_of(i, pair=pair):
                lo, hi = VIDEO_SELF[2 * pair + i]
                shift = (1 - 2 * pair - i) * B
                return self_bias[h, 0, lo + shift : hi + shift, :]

            tasks.append(
                task(q, kvn, vvt, part, self_of, functools.partial(video_done, pair, 0))
            )
            part = VIDEO_CROSS[2 * pair : 2 * pair + 2]

            def cross_of(i, pair=pair):
                lo, hi = VIDEO_CROSS[2 * pair + i]
                return va_bias[2 * pair + i, 0 : hi - lo, :]

            tasks.append(
                task(q, kan, vat, part, cross_of, functools.partial(video_done, pair, 1))
            )
        tasks.append(
            task(
                qan[...], kvn, vvt, AUDIO_CROSS,
                lambda j: av_bias[j, 0 : AUDIO_CROSS[j][1] - AUDIO_CROSS[j][0], :],
                functools.partial(audio_done, 0),
            )
        )
        tasks.append(
            task(
                qan[...], kan, vat, AUDIO_SELF,
                lambda j: self_bias[h, 1, (1 - j) * B : (3 - j) * B, :],
                functools.partial(audio_done, 1),
            )
        )
        in_turn(tasks)
        for side in (0, 1):
            qe[h, side, :B, :] = qvn[3 * side * B : (3 * side + 1) * B, :]
            qe[h, side, B:, :] = qan[side * B : (side + 1) * B, :]
        return carry

    lax.fori_loop(0, heads, own_keys, 0)

    no_left = jnp.where(me == 0, NEG, 0.0).astype(jnp.float32)
    no_right = jnp.where(me == n_tm - 1, NEG, 0.0).astype(jnp.float32)
    for side in (0, 1):
        pl.when(comes_from[side])(to_neighbours[side].wait_recv)
    for side in (0, 1):
        none = no_left if side == 0 else no_right
        hcol[side, 0] = column(nbr[side, 0:1, :])
        hcol[side, 1] = column(nbr[side, 1:2, :])
        acol = column(nbr[side, 2:3, :])
        vah_bias[side] = near(acol, colsf + (v0 + 3 * side * B)) + none
        avh_bias[side] = near(al[side : side + 1, :], rowsf + (v0 + (-B if side == 0 else 4 * B))) + none

    for side in (0, 1):
        pl.when(sends_to[side])(to_neighbours[side].wait_send)

    def neighbour_keys(h, carry):
        gains = [g[pl.ds(h, 1), :] for g in (gkv, gka)]
        total = {}

        def task(side, kind):
            none = no_left if side == 0 else no_right
            edge = slice(2 * side * B, (2 * side + 1) * B)
            reach = (HALO_AUDIO_CROSS, HALO_VIDEO_CROSS)[kind][side]
            cross = (avh_bias, vah_bias)[kind]
            row = 4 * side + 2 * kind
            held = {}

            def scores():
                keys = normed(halo[h, side, 2 * kind], hcol[side, kind], gains[kind])
                held["s"] = dot_nt(keys, qe[h, side])

            def weights():
                results = []
                for i in (0, 1):
                    lanes = slice(i * B, (i + 1) * B)
                    first, last = (0, B) if i == kind else reach
                    if i == kind:
                        bias = self_bias[h, kind, edge, :] + none
                    else:
                        bias = cross[side, first:last, :]
                    s = held["s"][first:last, lanes] + bias
                    m0 = ml[h, row : row + 1, lanes]
                    m = jnp.maximum(m0, jnp.max(s, axis=0, keepdims=True))
                    e = jnp.exp2((s - m) * C)
                    a = jnp.exp2((m0 - m) * C)
                    l = ml[h, row + 1 : row + 2, lanes] * a + jnp.sum(e, axis=0, keepdims=True)
                    results.append((a, l, padded(e.astype(jnp.bfloat16), first, B)))
                held["p"] = results

            def products():
                values = halo[h, side, 2 * kind + 1].T
                o = dot_nn(values, jnp.concatenate([p[2] for p in held["p"]], axis=1))
                for i in (0, 1):
                    lanes = slice(i * B, (i + 1) * B)
                    a, l, _ = held["p"][i]
                    total[kind, i] = (os[h, side, kind, :, lanes] * a + o[:, lanes]) * (1.0 / l)
                    if kind == 0:
                        os[h, side, kind, :, lanes] = total[kind, i]
                if kind == 1:
                    o = [os[h, side, 0, :, i * B : (i + 1) * B] + total[1, i] for i in (0, 1)]
                    part = slice(3 * side * B, (3 * side + 1) * B)
                    ov[part, columns(h)] = o[0].astype(jnp.bfloat16).T
                    part = slice(side * B, (side + 1) * B)
                    oa[part, columns(h)] = o[1].astype(jnp.bfloat16).T

            return scores, weights, products

        for kind in (0, 1):
            wait_halo(h, kind)
            in_turn([task(side, kind) for side in (0, 1)])
        return carry

    lax.fori_loop(0, heads, neighbour_keys, 0)


def move_kernel(a, b, x, y, sems):
    copies = [
        pltpu.make_async_copy(src, dst, sems.at[i]) for i, (src, dst) in enumerate(((a, x), (b, y)))
    ]
    for copy in copies:
        copy.start()
    for copy in copies:
        copy.wait()


def moved(arrays):
    vmem = pl.BlockSpec(memory_space=pltpu.VMEM)
    hbm = pl.BlockSpec(memory_space=pltpu.HBM)
    return pl.pallas_call(
        move_kernel,
        out_shape=tuple(jax.ShapeDtypeStruct(x.shape, x.dtype) for x in arrays),
        in_specs=[vmem, vmem],
        out_specs=(hbm, hbm),
        scratch_shapes=[pltpu.SemaphoreType.DMA((2,))],
        name="moved",
    )(*[pltpu.with_memory_space_constraint(x, pltpu.VMEM) for x in arrays])


def body(
    q_video, k_video, v_video, q_audio, k_audio, v_audio,
    q_gain_video, k_gain_video, q_gain_audio, k_gain_audio, audio_align, windows,
):
    n_tm = lax.axis_size("tm")
    rows_v, width = q_video.shape
    rows_a = q_audio.shape[0]
    heads = width // HEAD_DIM
    gains = [
        g.reshape(heads, HEAD_DIM) for g in (q_gain_video, k_gain_video, q_gain_audio, k_gain_audio)
    ]
    bf, f32 = jnp.bfloat16, jnp.float32
    vmem = pl.BlockSpec(memory_space=pltpu.VMEM)
    hbm = pl.BlockSpec(memory_space=pltpu.HBM)
    dma = pltpu.SemaphoreType.DMA
    results = pl.pallas_call(
        functools.partial(kernel, n_tm, heads),
        out_shape=(
            pltpu.VMEM(q_video.shape, bf),
            pltpu.VMEM(q_audio.shape, bf),
        ),
        in_specs=[pl.BlockSpec(memory_space=pltpu.SMEM)] + [hbm] * 11,
        out_specs=(vmem, vmem),
        scratch_shapes=[
            *[pltpu.VMEM((heads, B), f32) for _ in range(4)],
            pltpu.VMEM((rows_a // B, B), jnp.int32),
            pltpu.VMEM((heads, rows_v, B), bf),
            pltpu.VMEM((heads, rows_v, B), bf),
            pltpu.VMEM((heads, rows_v, B), bf),
            pltpu.VMEM((heads, rows_a, B), bf),
            pltpu.VMEM((heads, rows_a, B), bf),
            pltpu.VMEM((heads, rows_a, B), bf),
            pltpu.VMEM((heads, 2, 4, B, B), bf),
            pltpu.VMEM((4, 16, B), f32),
            pltpu.VMEM((2, 8, B), f32),
            pltpu.VMEM((2, 8, B), f32),
            pltpu.VMEM((12, B, B), f32),
            pltpu.VMEM((2, 2, B, B), f32),
            pltpu.VMEM((heads, 2, 3 * B, B), f32),
            pltpu.VMEM((4, 160, B), f32),
            pltpu.VMEM((2, 368, B), f32),
            pltpu.VMEM((2, B, B), f32),
            pltpu.VMEM((2, B, B), f32),
            pltpu.VMEM((rows_v, B), bf),
            pltpu.VMEM((rows_v, B), bf),
            pltpu.VMEM((rows_a, B), bf),
            pltpu.VMEM((rows_a, B), bf),
            pltpu.VMEM((heads, B, rows_v), bf),
            pltpu.VMEM((heads, B, rows_a), bf),
            pltpu.VMEM((heads, 2, 2 * B, B), bf),
            pltpu.VMEM((heads, 8, 2 * B), f32),
            pltpu.VMEM((heads, 2, 2, B, 2 * B), f32),
            dma((5,)),
            dma((6, heads)),
            dma((heads, 2, 4)),
            dma((heads, 2, 4)),
            dma((2,)),
            dma((2,)),
            dma((2,)),
            dma((2,)),
        ],
        compiler_params=pltpu.CompilerParams(
            collective_id=0, has_side_effects=True, vmem_limit_bytes=60 * 2**20
        ),
        name="attention",
    )(
        windows, *gains, audio_align.reshape(rows_a // B, B),
        q_video, k_video, v_video, q_audio, k_audio, v_audio,
    )
    return moved(results)


def solution(mesh):
    placed = (P("tm", "head"),) * 6 + (P("head"),) * 4 + (P("tm"), P(None, "head"))
    return jax.shard_map(
        body,
        mesh=mesh,
        in_specs=placed,
        out_specs=(P("tm", "head"), P("tm", "head")),
        check_vma=False,
    )
```

```python
import functools
import math

import jax
import jax.numpy as jnp
from jax import lax
from jax.experimental import pallas as pl
from jax.experimental.pallas import tpu as pltpu
from jax.sharding import PartitionSpec as P

HEAD_DIM = 128
D = 3072
WC = 64
EPS = 1e-06
B = 128
NEG = -1e30
C = math.log2(math.e) / math.sqrt(HEAD_DIM)
MESH = pl.DeviceIdType.MESH

ROW_QV, ROW_KV, ROW_QA, ROW_KA = 0, 4, 8, 10

VIDEO_SELF = ((0, 256), (0, 384), (128, 512), (256, 512))
VIDEO_CROSS = ((0, 96), (0, 160), (64, 224), (128, 256))
AUDIO_SELF = ((0, 256), (0, 256))
AUDIO_CROSS = ((0, 368), (192, 512))
HALO_VIDEO_CROSS = ((64, 128), (0, 32))
HALO_AUDIO_CROSS = ((64, 128), (0, 112))


def dot_nt(a, b):
    return lax.dot_general(a, b, (((1,), (1,)), ((), ())), preferred_element_type=jnp.float32)


def dot_nn(a, b):
    return jnp.dot(a, b, preferred_element_type=jnp.float32)


def column(row):
    return jnp.broadcast_to(row, (B, B)).T


def softened(s):
    m = jnp.max(s, axis=0, keepdims=True)
    e = jnp.exp2((s - m) * C)
    return m, jnp.sum(e, axis=0, keepdims=True), e.astype(jnp.bfloat16)


def padded(p, first, rows):
    last = rows - first - p.shape[0]
    parts = [jnp.zeros((first, B), p.dtype)] if first else []
    parts.append(p)
    if last:
        parts.append(jnp.zeros((last, B), p.dtype))
    return jnp.concatenate(parts, axis=0) if len(parts) > 1 else p


def in_turn(tasks):
    n = len(tasks)
    tasks[0][0]()
    for i in range(n):
        if i + 1 < n:
            tasks[i + 1][0]()
        tasks[i][1]()
        if i > 0:
            tasks[i - 1][2]()
    tasks[n - 1][2]()


def kernel(
    n_tm, heads,
    windows_hbm, gqv_hbm, gkv_hbm, gqa_hbm, gka_hbm, align_hbm,
    qv_hbm, kv_hbm, vv_hbm, qa_hbm, ka_hbm, va_hbm,
    ov, oa,
    windows, gqv, gkv, gqa, gka, align, qv, kv, vv, qa, ka, va, halo,
    sums, nb, nbr, fcol, hcol,
    self_bias, va_bias, av_bias, vah_bias, avh_bias,
    qvn, kvn, qan, kan, vvt, vat, qe, ml, os,
    small_sem, load_sem, hsend, hrecv, ssend, srecv, nsend, nrecv,
):
    me = lax.axis_index("tm")
    hd = lax.axis_index("head")
    right = jnp.minimum(me + 1, n_tm - 1)
    left = jnp.maximum(me - 1, 0)
    has_left = me > 0
    has_right = me < n_tm - 1
    sends_to = (has_right, has_left)
    comes_from = (has_left, has_right)
    peers = [lax.bitwise_xor(hd, 1), lax.bitwise_xor(hd, 2)]
    sources = (kv_hbm, vv_hbm, ka_hbm, va_hbm)
    loads = ((qv_hbm, qv), (kv_hbm, kv), (qa_hbm, qa), (ka_hbm, ka), (vv_hbm, vv), (va_hbm, va))

    def columns(h):
        start = h * HEAD_DIM
        return pl.ds(start if isinstance(h, int) else pl.multiple_of(start, HEAD_DIM), HEAD_DIM)

    def load(i, h):
        src, dst = loads[i]
        return pltpu.make_async_copy(src.at[:, columns(h)], dst.at[h], load_sem.at[i, h])

    small = [
        pltpu.make_async_copy(src, dst, small_sem.at[i])
        for i, (src, dst) in enumerate(
            ((align_hbm, align), (gqv_hbm, gqv), (gkv_hbm, gkv), (gqa_hbm, gqa), (gka_hbm, gka),
             (windows_hbm, windows))
        )
    ]

    def halo_copy(h, side, a):
        src = sources[a]
        row = src.shape[0] - B if side == 0 else 0
        return pltpu.make_async_remote_copy(
            src_ref=src.at[pl.ds(row, B), columns(h)],
            dst_ref=halo.at[h, side, a],
            send_sem=hsend.at[h, side, a],
            recv_sem=hrecv.at[h, side, a],
            device_id=(right if side == 0 else left, hd),
            device_id_type=MESH,
        )

    def start_halo(h, kinds=(0, 1)):
        for kind in kinds:
            for side in (0, 1):

                @pl.when(sends_to[side])
                def _():
                    for a in (2 * kind, 2 * kind + 1):
                        halo_copy(h, side, a).start()

    def wait_halo(h, kind):
        for side in (0, 1):

            @pl.when(sends_to[side])
            def _():
                for a in (2 * kind, 2 * kind + 1):
                    halo_copy(h, side, a).wait_send()

        for side in (0, 1):

            @pl.when(comes_from[side])
            def _():
                for a in (2 * kind, 2 * kind + 1):
                    halo_copy(h, side, a).wait_recv()

    sums[0] = jnp.zeros((16, B), jnp.float32)
    nb[...] = jnp.zeros_like(nb)
    barrier = pltpu.get_barrier_semaphore()
    for p in peers:
        pl.semaphore_signal(barrier, inc=1, device_id=(me, p), device_id_type=MESH)
    for there, device in ((has_right, right), (has_left, left)):

        @pl.when(there)
        def _():
            pl.semaphore_signal(barrier, inc=1, device_id=(device, hd), device_id_type=MESH)

    for i in range(4):
        for h in range(heads):
            load(i, h).start()
    for copy in small:
        copy.start()
    for i in (4, 5):
        for h in range(heads):
            load(i, h).start()
    for slot in (0, 1):

        @pl.when(jnp.logical_not(comes_from[slot]))
        def _():
            nbr[slot] = jnp.zeros((8, B), jnp.float32)

            def clear(h, carry):
                halo[h, slot] = jnp.zeros((4, B, B), jnp.bfloat16)
                return carry

            lax.fori_loop(0, heads, clear, 0)

    pl.semaphore_wait(
        barrier, 2 + has_left.astype(jnp.int32) + has_right.astype(jnp.int32)
    )
    start_halo(0, (0,))

    for i in range(4):
        for h in range(heads):
            load(i, h).wait()
    for ref, row in ((qv, ROW_QV), (kv, ROW_KV), (qa, ROW_QA), (ka, ROW_KA)):
        for r in range(ref.shape[1] // B):
            total = None
            for h in range(heads):
                x = ref[h, r * B : (r + 1) * B, :].astype(jnp.float32)
                total = x * x if total is None else total + x * x
            sums[0, row + r : row + r + 1, :] = jnp.sum(total.T, axis=0, keepdims=True)
    exchange = [
        pltpu.make_async_remote_copy(
            src_ref=sums.at[2 * i],
            dst_ref=sums.at[2 * i + 1],
            send_sem=ssend.at[i],
            recv_sem=srecv.at[i],
            device_id=(me, p),
            device_id_type=MESH,
        )
        for i, p in enumerate(peers)
    ]
    exchange[0].start()
    start_halo(0, (1,))

    for copy in small:
        copy.wait()
    v0 = (me * qv.shape[1]).astype(jnp.float32)
    al = align[...].astype(jnp.float32)
    rows = lax.broadcasted_iota(jnp.int32, (B, B), 0)
    cols = lax.broadcasted_iota(jnp.int32, (B, B), 1)
    rowsf = rows.astype(jnp.float32)
    colsf = cols.astype(jnp.float32)

    def near(x, y):
        return jnp.where(jnp.abs(x - y) <= WC, 0.0, NEG).astype(jnp.float32)

    acols = [column(al[j : j + 1, :]) for j in range(2)]
    for b, (lo, hi) in enumerate(VIDEO_CROSS):
        for t in range(lo // B, -(-hi // B)):
            first, last = max(lo, t * B), min(hi, (t + 1) * B)
            bias = near(acols[t], colsf + (v0 + b * B))
            va_bias[b, first - lo : last - lo, :] = bias[first - t * B : last - t * B, :]
    for j, (lo, hi) in enumerate(AUDIO_CROSS):
        for t in range(lo // B, -(-hi // B)):
            first, last = max(lo, t * B), min(hi, (t + 1) * B)
            bias = near(al[j : j + 1, :], rowsf + (v0 + t * B))
            av_bias[j, first - lo : last - lo, :] = bias[first - t * B : last - t * B, :]

    for i in (4, 5):
        for h in range(heads):
            load(i, h).wait()

    exchange[0].wait()
    sums[2] = sums[0] + sums[1]
    exchange[1].start()
    start_halo(1)
    start_halo(2)

    def turn_values(h, carry):
        for src, dst in ((vv, vvt), (va, vat)):
            for r in range(src.shape[1] // B):
                dst[h, :, r * B : (r + 1) * B] = src[h, r * B : (r + 1) * B, :].T
        return carry

    lax.fori_loop(0, heads, turn_values, 0)

    exchange[1].wait()
    factors = lax.rsqrt((sums[2] + sums[3]) / D + EPS)
    for side, picked in enumerate(((ROW_KV + 3, ROW_KA + 1, 1), (ROW_KV, ROW_KA, 0))):
        for i, row in enumerate(picked):
            source = factors if i < 2 else al
            nb[side, i : i + 1, :] = source[row : row + 1, :]
    to_neighbours = [
        pltpu.make_async_remote_copy(
            src_ref=nb.at[side],
            dst_ref=nbr.at[side],
            send_sem=nsend.at[side],
            recv_sem=nrecv.at[side],
            device_id=(right if side == 0 else left, hd),
            device_id_type=MESH,
        )
        for side in (0, 1)
    ]
    for side in (0, 1):
        pl.when(sends_to[side])(to_neighbours[side].start)
    for h in range(3, heads):
        start_halo(h)
    for c in range(12):
        fcol[c] = column(factors[c : c + 1, :])

    def normed(x, factor, gain):
        return (x.astype(jnp.float32) * factor * gain).astype(jnp.bfloat16)

    def own_keys(h, carry):
        gains = [g[pl.ds(h, 1), :] for g in (gqv, gkv, gqa, gka)]

        for src, dst, row, g in (
            (qv, qvn, ROW_QV, 0), (kv, kvn, ROW_KV, 1), (qa, qan, ROW_QA, 2), (ka, kan, ROW_KA, 3),
        ):
            for r in range(src.shape[1] // B):
                part = slice(r * B, (r + 1) * B)
                dst[part, :] = normed(src[h, part, :], fcol[row + r], gains[g])
        for kind in (0, 1):
            w = windows[kind, h]
            for t in range(3):
                far = jnp.abs(rows - cols + (t - 1) * B)
                self_bias[h, kind, t * B : (t + 1) * B, :] = jnp.where(far <= w, 0.0, NEG).astype(
                    jnp.float32
                )

        def keep(side, kind, half, m, l, o):
            lanes = slice(half * B, (half + 1) * B)
            row = 4 * side + 2 * kind
            ml[h, row : row + 1, lanes] = m
            ml[h, row + 1 : row + 2, lanes] = l
            os[h, side, kind, :, lanes] = o

        def task(queries, keys, values, windows_of, bias_of, finish):
            lo = min(w[0] for w in windows_of)
            hi = max(w[1] for w in windows_of)
            held = {}

            def scores():
                s = dot_nt(keys[lo:hi, :], queries)
                held["s"] = [
                    s[first - lo : last - lo, i * B : (i + 1) * B]
                    for i, (first, last) in enumerate(windows_of)
                ]

            def weights():
                held["p"] = [softened(held["s"][i] + bias_of(i)) for i in (0, 1)]

            def products():
                p = [
                    padded(held["p"][i][2], windows_of[i][0] - lo, hi - lo) for i in (0, 1)
                ]
                o = dot_nn(values[h, :, lo:hi], jnp.concatenate(p, axis=1))
                finish([(*held["p"][i][:2], o[:, i * B : (i + 1) * B]) for i in (0, 1)])

            return scores, weights, products

        done = {}

        def video_done(pair, kind, results):
            done[pair, kind] = results
            if (pair, 1 - kind) not in done:
                return
            for i in (0, 1):
                b = 2 * pair + i
                if b in (1, 2):
                    o = sum(done[pair, k][i][2] * (1.0 / done[pair, k][i][1]) for k in (0, 1))
                    ov[b * B : (b + 1) * B, columns(h)] = o.astype(jnp.bfloat16).T
                else:
                    for k in (0, 1):
                        keep(pair, k, 0, *done[pair, k][i])

        def audio_done(kind, results):
            for side in (0, 1):
                keep(side, kind, 1, *results[side])

        tasks = []
        for pair in (0, 1):
            q = qvn[2 * pair * B : 2 * (pair + 1) * B, :]
            part = VIDEO_SELF[2 * pair : 2 * pair + 2]

            def self_of(i, pair=pair):
                lo, hi = VIDEO_SELF[2 * pair + i]
                shift = (1 - 2 * pair - i) * B
                return self_bias[h, 0, lo + shift : hi + shift, :]

            tasks.append(
                task(q, kvn, vvt, part, self_of, functools.partial(video_done, pair, 0))
            )
            part = VIDEO_CROSS[2 * pair : 2 * pair + 2]

            def cross_of(i, pair=pair):
                lo, hi = VIDEO_CROSS[2 * pair + i]
                return va_bias[2 * pair + i, 0 : hi - lo, :]

            tasks.append(
                task(q, kan, vat, part, cross_of, functools.partial(video_done, pair, 1))
            )
        tasks.append(
            task(
                qan[...], kvn, vvt, AUDIO_CROSS,
                lambda j: av_bias[j, 0 : AUDIO_CROSS[j][1] - AUDIO_CROSS[j][0], :],
                functools.partial(audio_done, 0),
            )
        )
        tasks.append(
            task(
                qan[...], kan, vat, AUDIO_SELF,
                lambda j: self_bias[h, 1, (1 - j) * B : (3 - j) * B, :],
                functools.partial(audio_done, 1),
            )
        )
        in_turn(tasks)
        for side in (0, 1):
            qe[h, side, :B, :] = qvn[3 * side * B : (3 * side + 1) * B, :]
            qe[h, side, B:, :] = qan[side * B : (side + 1) * B, :]
        return carry

    lax.fori_loop(0, heads, own_keys, 0)

    no_left = jnp.where(me == 0, NEG, 0.0).astype(jnp.float32)
    no_right = jnp.where(me == n_tm - 1, NEG, 0.0).astype(jnp.float32)
    for side in (0, 1):
        pl.when(comes_from[side])(to_neighbours[side].wait_recv)
    for side in (0, 1):
        none = no_left if side == 0 else no_right
        hcol[side, 0] = column(nbr[side, 0:1, :])
        hcol[side, 1] = column(nbr[side, 1:2, :])
        acol = column(nbr[side, 2:3, :])
        vah_bias[side] = near(acol, colsf + (v0 + 3 * side * B)) + none
        avh_bias[side] = near(al[side : side + 1, :], rowsf + (v0 + (-B if side == 0 else 4 * B))) + none

    for side in (0, 1):
        pl.when(sends_to[side])(to_neighbours[side].wait_send)

    def neighbour_keys(h, carry):
        gains = [g[pl.ds(h, 1), :] for g in (gkv, gka)]
        total = {}

        def task(side, kind):
            none = no_left if side == 0 else no_right
            edge = slice(2 * side * B, (2 * side + 1) * B)
            reach = (HALO_AUDIO_CROSS, HALO_VIDEO_CROSS)[kind][side]
            cross = (avh_bias, vah_bias)[kind]
            row = 4 * side + 2 * kind
            held = {}

            def scores():
                keys = normed(halo[h, side, 2 * kind], hcol[side, kind], gains[kind])
                held["s"] = dot_nt(keys, qe[h, side])

            def weights():
                results = []
                for i in (0, 1):
                    lanes = slice(i * B, (i + 1) * B)
                    first, last = (0, B) if i == kind else reach
                    if i == kind:
                        bias = self_bias[h, kind, edge, :] + none
                    else:
                        bias = cross[side, first:last, :]
                    s = held["s"][first:last, lanes] + bias
                    m0 = ml[h, row : row + 1, lanes]
                    m = jnp.maximum(m0, jnp.max(s, axis=0, keepdims=True))
                    e = jnp.exp2((s - m) * C)
                    a = jnp.exp2((m0 - m) * C)
                    l = ml[h, row + 1 : row + 2, lanes] * a + jnp.sum(e, axis=0, keepdims=True)
                    results.append((a, l, padded(e.astype(jnp.bfloat16), first, B)))
                held["p"] = results

            def products():
                values = halo[h, side, 2 * kind + 1].T
                o = dot_nn(values, jnp.concatenate([p[2] for p in held["p"]], axis=1))
                for i in (0, 1):
                    lanes = slice(i * B, (i + 1) * B)
                    a, l, _ = held["p"][i]
                    total[kind, i] = (os[h, side, kind, :, lanes] * a + o[:, lanes]) * (1.0 / l)
                    if kind == 0:
                        os[h, side, kind, :, lanes] = total[kind, i]
                if kind == 1:
                    o = [os[h, side, 0, :, i * B : (i + 1) * B] + total[1, i] for i in (0, 1)]
                    part = slice(3 * side * B, (3 * side + 1) * B)
                    ov[part, columns(h)] = o[0].astype(jnp.bfloat16).T
                    part = slice(side * B, (side + 1) * B)
                    oa[part, columns(h)] = o[1].astype(jnp.bfloat16).T

            return scores, weights, products

        for kind in (0, 1):
            wait_halo(h, kind)
            in_turn([task(side, kind) for side in (0, 1)])
        return carry

    lax.fori_loop(0, heads, neighbour_keys, 0)


def move_kernel(a, b, x, y, sems):
    copies = [
        pltpu.make_async_copy(src, dst, sems.at[i]) for i, (src, dst) in enumerate(((a, x), (b, y)))
    ]
    for copy in copies:
        copy.start()
    for copy in copies:
        copy.wait()


def moved(arrays):
    vmem = pl.BlockSpec(memory_space=pltpu.VMEM)
    hbm = pl.BlockSpec(memory_space=pltpu.HBM)
    return pl.pallas_call(
        move_kernel,
        out_shape=tuple(jax.ShapeDtypeStruct(x.shape, x.dtype) for x in arrays),
        in_specs=[vmem, vmem],
        out_specs=(hbm, hbm),
        scratch_shapes=[pltpu.SemaphoreType.DMA((2,))],
        name="moved",
    )(*[pltpu.with_memory_space_constraint(x, pltpu.VMEM) for x in arrays])


def body(
    q_video, k_video, v_video, q_audio, k_audio, v_audio,
    q_gain_video, k_gain_video, q_gain_audio, k_gain_audio, audio_align, windows,
):
    n_tm = lax.axis_size("tm")
    rows_v, width = q_video.shape
    rows_a = q_audio.shape[0]
    heads = width // HEAD_DIM
    gains = [
        g.reshape(heads, HEAD_DIM) for g in (q_gain_video, k_gain_video, q_gain_audio, k_gain_audio)
    ]
    bf, f32 = jnp.bfloat16, jnp.float32
    vmem = pl.BlockSpec(memory_space=pltpu.VMEM)
    hbm = pl.BlockSpec(memory_space=pltpu.HBM)
    dma = pltpu.SemaphoreType.DMA
    results = pl.pallas_call(
        functools.partial(kernel, n_tm, heads),
        out_shape=(
            pltpu.VMEM(q_video.shape, bf),
            pltpu.VMEM(q_audio.shape, bf),
        ),
        in_specs=[hbm] * 12,
        out_specs=(vmem, vmem),
        scratch_shapes=[
            pltpu.SMEM(windows.shape, jnp.int32),
            *[pltpu.VMEM((heads, B), f32) for _ in range(4)],
            pltpu.VMEM((rows_a // B, B), jnp.int32),
            pltpu.VMEM((heads, rows_v, B), bf),
            pltpu.VMEM((heads, rows_v, B), bf),
            pltpu.VMEM((heads, rows_v, B), bf),
            pltpu.VMEM((heads, rows_a, B), bf),
            pltpu.VMEM((heads, rows_a, B), bf),
            pltpu.VMEM((heads, rows_a, B), bf),
            pltpu.VMEM((heads, 2, 4, B, B), bf),
            pltpu.VMEM((4, 16, B), f32),
            pltpu.VMEM((2, 8, B), f32),
            pltpu.VMEM((2, 8, B), f32),
            pltpu.VMEM((12, B, B), f32),
            pltpu.VMEM((2, 2, B, B), f32),
            pltpu.VMEM((heads, 2, 3 * B, B), f32),
            pltpu.VMEM((4, 160, B), f32),
            pltpu.VMEM((2, 368, B), f32),
            pltpu.VMEM((2, B, B), f32),
            pltpu.VMEM((2, B, B), f32),
            pltpu.VMEM((rows_v, B), bf),
            pltpu.VMEM((rows_v, B), bf),
            pltpu.VMEM((rows_a, B), bf),
            pltpu.VMEM((rows_a, B), bf),
            pltpu.VMEM((heads, B, rows_v), bf),
            pltpu.VMEM((heads, B, rows_a), bf),
            pltpu.VMEM((heads, 2, 2 * B, B), bf),
            pltpu.VMEM((heads, 8, 2 * B), f32),
            pltpu.VMEM((heads, 2, 2, B, 2 * B), f32),
            dma((6,)),
            dma((6, heads)),
            dma((heads, 2, 4)),
            dma((heads, 2, 4)),
            dma((2,)),
            dma((2,)),
            dma((2,)),
            dma((2,)),
        ],
        compiler_params=pltpu.CompilerParams(
            collective_id=0, has_side_effects=True, vmem_limit_bytes=60 * 2**20
        ),
        name="attention",
    )(
        windows, *gains, audio_align.reshape(rows_a // B, B),
        q_video, k_video, v_video, q_audio, k_audio, v_audio,
    )
    return moved(results)


def solution(mesh):
    placed = (P("tm", "head"),) * 6 + (P("head"),) * 4 + (P("tm"), P(None, "head"))
    return jax.shard_map(
        body,
        mesh=mesh,
        in_specs=placed,
        out_specs=(P("tm", "head"), P("tm", "head")),
        check_vma=False,
    )
```

```python
import functools
import math

import jax
import jax.numpy as jnp
from jax import lax
from jax.experimental import pallas as pl
from jax.experimental.pallas import tpu as pltpu
from jax.sharding import PartitionSpec as P

HEAD_DIM = 128
D = 3072
WC = 64
EPS = 1e-06
B = 128
NEG = -1e30
C = math.log2(math.e) / math.sqrt(HEAD_DIM)
MESH = pl.DeviceIdType.MESH

ROW_QV, ROW_KV, ROW_QA, ROW_KA = 0, 4, 8, 10

VIDEO_SELF = ((0, 256), (0, 384), (128, 512), (256, 512))
VIDEO_CROSS = ((0, 96), (0, 160), (64, 224), (128, 256))
AUDIO_SELF = ((0, 256), (0, 256))
AUDIO_CROSS = ((0, 368), (192, 512))
HALO_VIDEO_CROSS = ((64, 128), (0, 32))
HALO_AUDIO_CROSS = ((64, 128), (0, 112))


def dot_nt(a, b):
    return lax.dot_general(a, b, (((1,), (1,)), ((), ())), preferred_element_type=jnp.float32)


def dot_nn(a, b):
    return jnp.dot(a, b, preferred_element_type=jnp.float32)


def column(row):
    return jnp.broadcast_to(row, (B, B)).T


def softened(s):
    m = jnp.max(s, axis=0, keepdims=True)
    e = jnp.exp2((s - m) * C)
    return m, jnp.sum(e, axis=0, keepdims=True), e.astype(jnp.bfloat16)


def padded(p, first, rows):
    last = rows - first - p.shape[0]
    parts = [jnp.zeros((first, B), p.dtype)] if first else []
    parts.append(p)
    if last:
        parts.append(jnp.zeros((last, B), p.dtype))
    return jnp.concatenate(parts, axis=0) if len(parts) > 1 else p


def in_turn(tasks):
    n = len(tasks)
    tasks[0][0]()
    for i in range(n):
        if i + 1 < n:
            tasks[i + 1][0]()
        tasks[i][1]()
        if i > 0:
            tasks[i - 1][2]()
    tasks[n - 1][2]()


def kernel(
    n_tm, heads,
    windows_hbm, gqv_hbm, gkv_hbm, gqa_hbm, gka_hbm, align_hbm,
    qv_hbm, kv_hbm, vv_hbm, qa_hbm, ka_hbm, va_hbm,
    ov, oa,
    windows, gqv, gkv, gqa, gka, align, qv, kv, vv, qa, ka, va, halo,
    sums, nb, nbr, fcol, hcol,
    self_bias, va_bias, av_bias, vah_bias, avh_bias,
    qvn, kvn, qan, kan, vvt, vat, qe, ml, os,
    small_sem, load_sem, hsend, hrecv, ssend, srecv, nsend, nrecv,
):
    me = lax.axis_index("tm")
    hd = lax.axis_index("head")
    right = jnp.minimum(me + 1, n_tm - 1)
    left = jnp.maximum(me - 1, 0)
    has_left = me > 0
    has_right = me < n_tm - 1
    sends_to = (has_right, has_left)
    comes_from = (has_left, has_right)
    peers = [lax.bitwise_xor(hd, 1), lax.bitwise_xor(hd, 2)]
    sources = (kv_hbm, vv_hbm, ka_hbm, va_hbm)
    loads = ((qv_hbm, qv), (kv_hbm, kv), (qa_hbm, qa), (ka_hbm, ka), (vv_hbm, vv), (va_hbm, va))

    def columns(h):
        start = h * HEAD_DIM
        return pl.ds(start if isinstance(h, int) else pl.multiple_of(start, HEAD_DIM), HEAD_DIM)

    def load(i, h):
        src, dst = loads[i]
        return pltpu.make_async_copy(src.at[:, columns(h)], dst.at[h], load_sem.at[i, h])

    small = [
        pltpu.make_async_copy(src, dst, small_sem.at[i])
        for i, (src, dst) in enumerate(
            ((align_hbm, align), (gqv_hbm, gqv), (gkv_hbm, gkv), (gqa_hbm, gqa), (gka_hbm, gka),
             (windows_hbm, windows))
        )
    ]

    def halo_copy(h, side, a):
        src = sources[a]
        row = src.shape[0] - B if side == 0 else 0
        return pltpu.make_async_remote_copy(
            src_ref=src.at[pl.ds(row, B), columns(h)],
            dst_ref=halo.at[h, side, a],
            send_sem=hsend.at[h, side, a],
            recv_sem=hrecv.at[h, side, a],
            device_id=(right if side == 0 else left, hd),
            device_id_type=MESH,
        )

    def start_halo(h, kinds=(0, 1)):
        for kind in kinds:
            for a in (2 * kind, 2 * kind + 1):
                for side in (0, 1):
                    pl.when(sends_to[side])(halo_copy(h, side, a).start)

    def wait_halo(h, a):
        for side in (0, 1):
            pl.when(sends_to[side])(halo_copy(h, side, a).wait_send)
        for side in (0, 1):
            pl.when(comes_from[side])(halo_copy(h, side, a).wait_recv)

    sums[0] = jnp.zeros((16, B), jnp.float32)
    nb[...] = jnp.zeros_like(nb)
    barrier = pltpu.get_barrier_semaphore()
    for p in peers:
        pl.semaphore_signal(barrier, inc=1, device_id=(me, p), device_id_type=MESH)
    for there, device in ((has_right, right), (has_left, left)):

        @pl.when(there)
        def _():
            pl.semaphore_signal(barrier, inc=1, device_id=(device, hd), device_id_type=MESH)

    for i in range(4):
        for h in range(heads):
            load(i, h).start()
    for copy in small:
        copy.start()
    for i in (4, 5):
        for h in range(heads):
            load(i, h).start()
    for slot in (0, 1):

        @pl.when(jnp.logical_not(comes_from[slot]))
        def _():
            nbr[slot] = jnp.zeros((8, B), jnp.float32)

            def clear(h, carry):
                halo[h, slot] = jnp.zeros((4, B, B), jnp.bfloat16)
                return carry

            lax.fori_loop(0, heads, clear, 0)

    pl.semaphore_wait(
        barrier, 2 + has_left.astype(jnp.int32) + has_right.astype(jnp.int32)
    )
    start_halo(0, (0,))

    for i in range(4):
        for h in range(heads):
            load(i, h).wait()
    for ref, row in ((qv, ROW_QV), (kv, ROW_KV), (qa, ROW_QA), (ka, ROW_KA)):
        for r in range(ref.shape[1] // B):
            total = None
            for h in range(heads):
                x = ref[h, r * B : (r + 1) * B, :].astype(jnp.float32)
                total = x * x if total is None else total + x * x
            sums[0, row + r : row + r + 1, :] = jnp.sum(total.T, axis=0, keepdims=True)
    exchange = [
        pltpu.make_async_remote_copy(
            src_ref=sums.at[2 * i],
            dst_ref=sums.at[2 * i + 1],
            send_sem=ssend.at[i],
            recv_sem=srecv.at[i],
            device_id=(me, p),
            device_id_type=MESH,
        )
        for i, p in enumerate(peers)
    ]
    exchange[0].start()
    start_halo(0, (1,))

    for copy in small:
        copy.wait()
    v0 = (me * qv.shape[1]).astype(jnp.float32)
    al = align[...].astype(jnp.float32)
    rows = lax.broadcasted_iota(jnp.int32, (B, B), 0)
    cols = lax.broadcasted_iota(jnp.int32, (B, B), 1)
    rowsf = rows.astype(jnp.float32)
    colsf = cols.astype(jnp.float32)

    def near(x, y):
        return jnp.where(jnp.abs(x - y) <= WC, 0.0, NEG).astype(jnp.float32)

    acols = [column(al[j : j + 1, :]) for j in range(2)]
    for b, (lo, hi) in enumerate(VIDEO_CROSS):
        for t in range(lo // B, -(-hi // B)):
            first, last = max(lo, t * B), min(hi, (t + 1) * B)
            bias = near(acols[t], colsf + (v0 + b * B))
            va_bias[b, first - lo : last - lo, :] = bias[first - t * B : last - t * B, :]
    for j, (lo, hi) in enumerate(AUDIO_CROSS):
        for t in range(lo // B, -(-hi // B)):
            first, last = max(lo, t * B), min(hi, (t + 1) * B)
            bias = near(al[j : j + 1, :], rowsf + (v0 + t * B))
            av_bias[j, first - lo : last - lo, :] = bias[first - t * B : last - t * B, :]

    for i in (4, 5):
        for h in range(heads):
            load(i, h).wait()

    exchange[0].wait()
    sums[2] = sums[0] + sums[1]
    exchange[1].start()
    start_halo(1)
    start_halo(2)

    def turn_values(h, carry):
        for src, dst in ((vv, vvt), (va, vat)):
            for r in range(src.shape[1] // B):
                dst[h, :, r * B : (r + 1) * B] = src[h, r * B : (r + 1) * B, :].T
        return carry

    lax.fori_loop(0, heads, turn_values, 0)

    exchange[1].wait()
    factors = lax.rsqrt((sums[2] + sums[3]) / D + EPS)
    for side, picked in enumerate(((ROW_KV + 3, ROW_KA + 1, 1), (ROW_KV, ROW_KA, 0))):
        for i, row in enumerate(picked):
            source = factors if i < 2 else al
            nb[side, i : i + 1, :] = source[row : row + 1, :]
    to_neighbours = [
        pltpu.make_async_remote_copy(
            src_ref=nb.at[side],
            dst_ref=nbr.at[side],
            send_sem=nsend.at[side],
            recv_sem=nrecv.at[side],
            device_id=(right if side == 0 else left, hd),
            device_id_type=MESH,
        )
        for side in (0, 1)
    ]
    for side in (0, 1):
        pl.when(sends_to[side])(to_neighbours[side].start)
    for h in range(3, heads):
        start_halo(h)
    for c in range(12):
        fcol[c] = column(factors[c : c + 1, :])

    def normed(x, factor, gain):
        return (x.astype(jnp.float32) * factor * gain).astype(jnp.bfloat16)

    def own_keys(h, carry):
        gains = [g[pl.ds(h, 1), :] for g in (gqv, gkv, gqa, gka)]

        for src, dst, row, g in (
            (qv, qvn, ROW_QV, 0), (kv, kvn, ROW_KV, 1), (qa, qan, ROW_QA, 2), (ka, kan, ROW_KA, 3),
        ):
            for r in range(src.shape[1] // B):
                part = slice(r * B, (r + 1) * B)
                dst[part, :] = normed(src[h, part, :], fcol[row + r], gains[g])
        for kind in (0, 1):
            w = windows[kind, h]
            for t in range(3):
                far = jnp.abs(rows - cols + (t - 1) * B)
                self_bias[h, kind, t * B : (t + 1) * B, :] = jnp.where(far <= w, 0.0, NEG).astype(
                    jnp.float32
                )

        def keep(side, kind, half, m, l, o):
            lanes = slice(half * B, (half + 1) * B)
            row = 4 * side + 2 * kind
            ml[h, row : row + 1, lanes] = m
            ml[h, row + 1 : row + 2, lanes] = l
            os[h, side, kind, :, lanes] = o

        def task(queries, keys, values, windows_of, bias_of, finish):
            lo = min(w[0] for w in windows_of)
            hi = max(w[1] for w in windows_of)
            held = {}

            def scores():
                s = dot_nt(keys[lo:hi, :], queries)
                held["s"] = [
                    s[first - lo : last - lo, i * B : (i + 1) * B]
                    for i, (first, last) in enumerate(windows_of)
                ]

            def weights():
                held["p"] = [softened(held["s"][i] + bias_of(i)) for i in (0, 1)]

            def products():
                p = [
                    padded(held["p"][i][2], windows_of[i][0] - lo, hi - lo) for i in (0, 1)
                ]
                o = dot_nn(values[h, :, lo:hi], jnp.concatenate(p, axis=1))
                finish([(*held["p"][i][:2], o[:, i * B : (i + 1) * B]) for i in (0, 1)])

            return scores, weights, products

        done = {}

        def video_done(pair, kind, results):
            done[pair, kind] = results
            if (pair, 1 - kind) not in done:
                return
            for i in (0, 1):
                b = 2 * pair + i
                if b in (1, 2):
                    o = sum(done[pair, k][i][2] * (1.0 / done[pair, k][i][1]) for k in (0, 1))
                    ov[b * B : (b + 1) * B, columns(h)] = o.astype(jnp.bfloat16).T
                else:
                    for k in (0, 1):
                        keep(pair, k, 0, *done[pair, k][i])

        def audio_done(kind, results):
            for side in (0, 1):
                keep(side, kind, 1, *results[side])

        tasks = []
        for pair in (0, 1):
            q = qvn[2 * pair * B : 2 * (pair + 1) * B, :]
            part = VIDEO_SELF[2 * pair : 2 * pair + 2]

            def self_of(i, pair=pair):
                lo, hi = VIDEO_SELF[2 * pair + i]
                shift = (1 - 2 * pair - i) * B
                return self_bias[h, 0, lo + shift : hi + shift, :]

            tasks.append(
                task(q, kvn, vvt, part, self_of, functools.partial(video_done, pair, 0))
            )
            part = VIDEO_CROSS[2 * pair : 2 * pair + 2]

            def cross_of(i, pair=pair):
                lo, hi = VIDEO_CROSS[2 * pair + i]
                return va_bias[2 * pair + i, 0 : hi - lo, :]

            tasks.append(
                task(q, kan, vat, part, cross_of, functools.partial(video_done, pair, 1))
            )
        tasks.append(
            task(
                qan[...], kvn, vvt, AUDIO_CROSS,
                lambda j: av_bias[j, 0 : AUDIO_CROSS[j][1] - AUDIO_CROSS[j][0], :],
                functools.partial(audio_done, 0),
            )
        )
        tasks.append(
            task(
                qan[...], kan, vat, AUDIO_SELF,
                lambda j: self_bias[h, 1, (1 - j) * B : (3 - j) * B, :],
                functools.partial(audio_done, 1),
            )
        )
        in_turn(tasks)
        for side in (0, 1):
            qe[h, side, :B, :] = qvn[3 * side * B : (3 * side + 1) * B, :]
            qe[h, side, B:, :] = qan[side * B : (side + 1) * B, :]
        return carry

    lax.fori_loop(0, heads, own_keys, 0)

    no_left = jnp.where(me == 0, NEG, 0.0).astype(jnp.float32)
    no_right = jnp.where(me == n_tm - 1, NEG, 0.0).astype(jnp.float32)
    for side in (0, 1):
        pl.when(comes_from[side])(to_neighbours[side].wait_recv)
    for side in (0, 1):
        none = no_left if side == 0 else no_right
        hcol[side, 0] = column(nbr[side, 0:1, :])
        hcol[side, 1] = column(nbr[side, 1:2, :])
        acol = column(nbr[side, 2:3, :])
        vah_bias[side] = near(acol, colsf + (v0 + 3 * side * B)) + none
        avh_bias[side] = near(al[side : side + 1, :], rowsf + (v0 + (-B if side == 0 else 4 * B))) + none

    for side in (0, 1):
        pl.when(sends_to[side])(to_neighbours[side].wait_send)

    def neighbour_keys(h, carry):
        gains = [g[pl.ds(h, 1), :] for g in (gkv, gka)]
        total = {}

        def task(side, kind):
            none = no_left if side == 0 else no_right
            edge = slice(2 * side * B, (2 * side + 1) * B)
            reach = (HALO_AUDIO_CROSS, HALO_VIDEO_CROSS)[kind][side]
            cross = (avh_bias, vah_bias)[kind]
            row = 4 * side + 2 * kind
            held = {}

            def scores():
                keys = normed(halo[h, side, 2 * kind], hcol[side, kind], gains[kind])
                held["s"] = dot_nt(keys, qe[h, side])

            def weights():
                results = []
                for i in (0, 1):
                    lanes = slice(i * B, (i + 1) * B)
                    first, last = (0, B) if i == kind else reach
                    if i == kind:
                        bias = self_bias[h, kind, edge, :] + none
                    else:
                        bias = cross[side, first:last, :]
                    s = held["s"][first:last, lanes] + bias
                    m0 = ml[h, row : row + 1, lanes]
                    m = jnp.maximum(m0, jnp.max(s, axis=0, keepdims=True))
                    e = jnp.exp2((s - m) * C)
                    a = jnp.exp2((m0 - m) * C)
                    l = ml[h, row + 1 : row + 2, lanes] * a + jnp.sum(e, axis=0, keepdims=True)
                    results.append((a, l, padded(e.astype(jnp.bfloat16), first, B)))
                held["p"] = results

            def products():
                values = halo[h, side, 2 * kind + 1].T
                o = dot_nn(values, jnp.concatenate([p[2] for p in held["p"]], axis=1))
                for i in (0, 1):
                    lanes = slice(i * B, (i + 1) * B)
                    a, l, _ = held["p"][i]
                    total[kind, i] = (os[h, side, kind, :, lanes] * a + o[:, lanes]) * (1.0 / l)
                    if kind == 0:
                        os[h, side, kind, :, lanes] = total[kind, i]
                if kind == 1:
                    o = [os[h, side, 0, :, i * B : (i + 1) * B] + total[1, i] for i in (0, 1)]
                    part = slice(3 * side * B, (3 * side + 1) * B)
                    ov[part, columns(h)] = o[0].astype(jnp.bfloat16).T
                    part = slice(side * B, (side + 1) * B)
                    oa[part, columns(h)] = o[1].astype(jnp.bfloat16).T

            return scores, weights, products

        for kind in (0, 1):
            tasks = [task(side, kind) for side in (0, 1)]
            wait_halo(h, 2 * kind)
            for step in (0, 1):
                for steps in tasks:
                    steps[step]()
            wait_halo(h, 2 * kind + 1)
            for steps in tasks:
                steps[2]()
        return carry

    lax.fori_loop(0, heads, neighbour_keys, 0)


def move_kernel(a, b, x, y, sems):
    copies = [
        pltpu.make_async_copy(src, dst, sems.at[i]) for i, (src, dst) in enumerate(((a, x), (b, y)))
    ]
    for copy in copies:
        copy.start()
    for copy in copies:
        copy.wait()


def moved(arrays):
    vmem = pl.BlockSpec(memory_space=pltpu.VMEM)
    hbm = pl.BlockSpec(memory_space=pltpu.HBM)
    return pl.pallas_call(
        move_kernel,
        out_shape=tuple(jax.ShapeDtypeStruct(x.shape, x.dtype) for x in arrays),
        in_specs=[vmem, vmem],
        out_specs=(hbm, hbm),
        scratch_shapes=[pltpu.SemaphoreType.DMA((2,))],
        name="moved",
    )(*[pltpu.with_memory_space_constraint(x, pltpu.VMEM) for x in arrays])


def body(
    q_video, k_video, v_video, q_audio, k_audio, v_audio,
    q_gain_video, k_gain_video, q_gain_audio, k_gain_audio, audio_align, windows,
):
    n_tm = lax.axis_size("tm")
    rows_v, width = q_video.shape
    rows_a = q_audio.shape[0]
    heads = width // HEAD_DIM
    gains = [
        g.reshape(heads, HEAD_DIM) for g in (q_gain_video, k_gain_video, q_gain_audio, k_gain_audio)
    ]
    bf, f32 = jnp.bfloat16, jnp.float32
    vmem = pl.BlockSpec(memory_space=pltpu.VMEM)
    hbm = pl.BlockSpec(memory_space=pltpu.HBM)
    dma = pltpu.SemaphoreType.DMA
    results = pl.pallas_call(
        functools.partial(kernel, n_tm, heads),
        out_shape=(
            pltpu.VMEM(q_video.shape, bf),
            pltpu.VMEM(q_audio.shape, bf),
        ),
        in_specs=[hbm] * 12,
        out_specs=(vmem, vmem),
        scratch_shapes=[
            pltpu.SMEM(windows.shape, jnp.int32),
            *[pltpu.VMEM((heads, B), f32) for _ in range(4)],
            pltpu.VMEM((rows_a // B, B), jnp.int32),
            pltpu.VMEM((heads, rows_v, B), bf),
            pltpu.VMEM((heads, rows_v, B), bf),
            pltpu.VMEM((heads, rows_v, B), bf),
            pltpu.VMEM((heads, rows_a, B), bf),
            pltpu.VMEM((heads, rows_a, B), bf),
            pltpu.VMEM((heads, rows_a, B), bf),
            pltpu.VMEM((heads, 2, 4, B, B), bf),
            pltpu.VMEM((4, 16, B), f32),
            pltpu.VMEM((2, 8, B), f32),
            pltpu.VMEM((2, 8, B), f32),
            pltpu.VMEM((12, B, B), f32),
            pltpu.VMEM((2, 2, B, B), f32),
            pltpu.VMEM((heads, 2, 3 * B, B), f32),
            pltpu.VMEM((4, 160, B), f32),
            pltpu.VMEM((2, 368, B), f32),
            pltpu.VMEM((2, B, B), f32),
            pltpu.VMEM((2, B, B), f32),
            pltpu.VMEM((rows_v, B), bf),
            pltpu.VMEM((rows_v, B), bf),
            pltpu.VMEM((rows_a, B), bf),
            pltpu.VMEM((rows_a, B), bf),
            pltpu.VMEM((heads, B, rows_v), bf),
            pltpu.VMEM((heads, B, rows_a), bf),
            pltpu.VMEM((heads, 2, 2 * B, B), bf),
            pltpu.VMEM((heads, 8, 2 * B), f32),
            pltpu.VMEM((heads, 2, 2, B, 2 * B), f32),
            dma((6,)),
            dma((6, heads)),
            dma((heads, 2, 4)),
            dma((heads, 2, 4)),
            dma((2,)),
            dma((2,)),
            dma((2,)),
            dma((2,)),
        ],
        compiler_params=pltpu.CompilerParams(
            collective_id=0, has_side_effects=True, vmem_limit_bytes=60 * 2**20
        ),
        name="attention",
    )(
        windows, *gains, audio_align.reshape(rows_a // B, B),
        q_video, k_video, v_video, q_audio, k_audio, v_audio,
    )
    return moved(results)


def solution(mesh):
    placed = (P("tm", "head"),) * 6 + (P("head"),) * 4 + (P("tm"), P(None, "head"))
    return jax.shard_map(
        body,
        mesh=mesh,
        in_specs=placed,
        out_specs=(P("tm", "head"), P("tm", "head")),
        check_vma=False,
    )
```

```python
import functools
import math

import jax
import jax.numpy as jnp
from jax import lax
from jax.experimental import pallas as pl
from jax.experimental.pallas import tpu as pltpu
from jax.sharding import PartitionSpec as P

HEAD_DIM = 128
D = 3072
WC = 64
EPS = 1e-06
B = 128
NEG = -1e30
C = math.log2(math.e) / math.sqrt(HEAD_DIM)
MESH = pl.DeviceIdType.MESH

ROW_QV, ROW_KV, ROW_QA, ROW_KA = 0, 4, 8, 10

VIDEO_SELF = ((0, 256), (0, 384), (128, 512), (256, 512))
VIDEO_CROSS = ((0, 96), (0, 160), (64, 224), (128, 256))
AUDIO_SELF = ((0, 256), (0, 256))
AUDIO_CROSS = ((0, 368), (192, 512))
HALO_VIDEO_CROSS = ((64, 128), (0, 32))
HALO_AUDIO_CROSS = ((64, 128), (0, 112))


def dot_nt(a, b):
    return lax.dot_general(a, b, (((1,), (1,)), ((), ())), preferred_element_type=jnp.float32)


def dot_nn(a, b):
    return jnp.dot(a, b, preferred_element_type=jnp.float32)


def column(row):
    return jnp.broadcast_to(row, (B, B)).T


def softened(s):
    m = jnp.max(s, axis=0, keepdims=True)
    e = jnp.exp2((s - m) * C)
    return m, jnp.sum(e, axis=0, keepdims=True), e.astype(jnp.bfloat16)


def padded(p, first, rows):
    last = rows - first - p.shape[0]
    parts = [jnp.zeros((first, B), p.dtype)] if first else []
    parts.append(p)
    if last:
        parts.append(jnp.zeros((last, B), p.dtype))
    return jnp.concatenate(parts, axis=0) if len(parts) > 1 else p


def in_turn(tasks):
    n = len(tasks)
    tasks[0][0]()
    for i in range(n):
        if i + 1 < n:
            tasks[i + 1][0]()
        tasks[i][1]()
        if i > 0:
            tasks[i - 1][2]()
    tasks[n - 1][2]()


def kernel(
    n_tm, heads,
    windows_hbm, gqv_hbm, gkv_hbm, gqa_hbm, gka_hbm, align_hbm,
    qv_hbm, kv_hbm, vv_hbm, qa_hbm, ka_hbm, va_hbm,
    ov, oa,
    windows, gqv, gkv, gqa, gka, align, qv, kv, vv, qa, ka, va, halo,
    sums, nb, nbr, fcol, hcol,
    self_bias, va_bias, av_bias, vah_bias, avh_bias,
    qvn, kvn, qan, kan, vvt, vat, qe, ml, os,
    small_sem, load_sem, hsend, hrecv, ssend, srecv, nsend, nrecv,
):
    me = lax.axis_index("tm")
    hd = lax.axis_index("head")
    right = jnp.minimum(me + 1, n_tm - 1)
    left = jnp.maximum(me - 1, 0)
    has_left = me > 0
    has_right = me < n_tm - 1
    sends_to = (has_right, has_left)
    comes_from = (has_left, has_right)
    peers = [lax.bitwise_xor(hd, 1), lax.bitwise_xor(hd, 2)]
    sources = (kv_hbm, vv_hbm, ka_hbm, va_hbm)
    loads = ((qv_hbm, qv), (kv_hbm, kv), (qa_hbm, qa), (ka_hbm, ka), (vv_hbm, vv), (va_hbm, va))

    def columns(h):
        start = h * HEAD_DIM
        return pl.ds(start if isinstance(h, int) else pl.multiple_of(start, HEAD_DIM), HEAD_DIM)

    def load(i, h):
        src, dst = loads[i]
        return pltpu.make_async_copy(src.at[:, columns(h)], dst.at[h], load_sem.at[i, h])

    small = [
        pltpu.make_async_copy(src, dst, small_sem.at[i])
        for i, (src, dst) in enumerate(
            ((align_hbm, align), (gqv_hbm, gqv), (gkv_hbm, gkv), (gqa_hbm, gqa), (gka_hbm, gka),
             (windows_hbm, windows))
        )
    ]

    def halo_copy(h, side, a):
        src = sources[a]
        row = src.shape[0] - B if side == 0 else 0
        return pltpu.make_async_remote_copy(
            src_ref=src.at[pl.ds(row, B), columns(h)],
            dst_ref=halo.at[h, side, a],
            send_sem=hsend.at[h, side, a],
            recv_sem=hrecv.at[h, side, a],
            device_id=(right if side == 0 else left, hd),
            device_id_type=MESH,
        )

    def start_halo(h, kinds=(0, 1)):
        for kind in kinds:
            for a in (2 * kind, 2 * kind + 1):
                for side in (0, 1):
                    pl.when(sends_to[side])(halo_copy(h, side, a).start)

    def wait_halo(h, a):
        for side in (0, 1):
            pl.when(sends_to[side])(halo_copy(h, side, a).wait_send)
        for side in (0, 1):
            pl.when(comes_from[side])(halo_copy(h, side, a).wait_recv)

    sums[0] = jnp.zeros((16, B), jnp.float32)
    nb[...] = jnp.zeros_like(nb)
    barrier = pltpu.get_barrier_semaphore()
    for p in peers:
        pl.semaphore_signal(barrier, inc=1, device_id=(me, p), device_id_type=MESH)
    for there, device in ((has_right, right), (has_left, left)):

        @pl.when(there)
        def _():
            pl.semaphore_signal(barrier, inc=1, device_id=(device, hd), device_id_type=MESH)

    for i in range(4):
        for h in range(heads):
            load(i, h).start()
    for slot in (0, 1):

        @pl.when(jnp.logical_not(comes_from[slot]))
        def _():
            nbr[slot] = jnp.zeros((8, B), jnp.float32)

            def clear(h, carry):
                halo[h, slot] = jnp.zeros((4, B, B), jnp.bfloat16)
                return carry

            lax.fori_loop(0, heads, clear, 0)

    pl.semaphore_wait(
        barrier, 2 + has_left.astype(jnp.int32) + has_right.astype(jnp.int32)
    )
    start_halo(0, (0,))
    for copy in small:
        copy.start()
    for i in (4, 5):
        for h in range(heads):
            load(i, h).start()

    for i in range(4):
        for h in range(heads):
            load(i, h).wait()
    for ref, row in ((qv, ROW_QV), (kv, ROW_KV), (qa, ROW_QA), (ka, ROW_KA)):
        for r in range(ref.shape[1] // B):
            total = None
            for h in range(heads):
                x = ref[h, r * B : (r + 1) * B, :].astype(jnp.float32)
                total = x * x if total is None else total + x * x
            sums[0, row + r : row + r + 1, :] = jnp.sum(total.T, axis=0, keepdims=True)
    exchange = [
        pltpu.make_async_remote_copy(
            src_ref=sums.at[2 * i],
            dst_ref=sums.at[2 * i + 1],
            send_sem=ssend.at[i],
            recv_sem=srecv.at[i],
            device_id=(me, p),
            device_id_type=MESH,
        )
        for i, p in enumerate(peers)
    ]
    exchange[0].start()
    start_halo(0, (1,))

    for copy in small:
        copy.wait()
    v0 = (me * qv.shape[1]).astype(jnp.float32)
    al = align[...].astype(jnp.float32)
    rows = lax.broadcasted_iota(jnp.int32, (B, B), 0)
    cols = lax.broadcasted_iota(jnp.int32, (B, B), 1)
    rowsf = rows.astype(jnp.float32)
    colsf = cols.astype(jnp.float32)

    def near(x, y):
        return jnp.where(jnp.abs(x - y) <= WC, 0.0, NEG).astype(jnp.float32)

    acols = [column(al[j : j + 1, :]) for j in range(2)]
    for b, (lo, hi) in enumerate(VIDEO_CROSS):
        for t in range(lo // B, -(-hi // B)):
            first, last = max(lo, t * B), min(hi, (t + 1) * B)
            bias = near(acols[t], colsf + (v0 + b * B))
            va_bias[b, first - lo : last - lo, :] = bias[first - t * B : last - t * B, :]
    for j, (lo, hi) in enumerate(AUDIO_CROSS):
        for t in range(lo // B, -(-hi // B)):
            first, last = max(lo, t * B), min(hi, (t + 1) * B)
            bias = near(al[j : j + 1, :], rowsf + (v0 + t * B))
            av_bias[j, first - lo : last - lo, :] = bias[first - t * B : last - t * B, :]

    for i in (4, 5):
        for h in range(heads):
            load(i, h).wait()

    exchange[0].wait()
    sums[2] = sums[0] + sums[1]
    exchange[1].start()
    start_halo(1)
    start_halo(2)

    def turn_values(h, carry):
        for src, dst in ((vv, vvt), (va, vat)):
            for r in range(src.shape[1] // B):
                dst[h, :, r * B : (r + 1) * B] = src[h, r * B : (r + 1) * B, :].T
        return carry

    lax.fori_loop(0, heads, turn_values, 0)

    exchange[1].wait()
    factors = lax.rsqrt((sums[2] + sums[3]) / D + EPS)
    for side, picked in enumerate(((ROW_KV + 3, ROW_KA + 1, 1), (ROW_KV, ROW_KA, 0))):
        for i, row in enumerate(picked):
            source = factors if i < 2 else al
            nb[side, i : i + 1, :] = source[row : row + 1, :]
    to_neighbours = [
        pltpu.make_async_remote_copy(
            src_ref=nb.at[side],
            dst_ref=nbr.at[side],
            send_sem=nsend.at[side],
            recv_sem=nrecv.at[side],
            device_id=(right if side == 0 else left, hd),
            device_id_type=MESH,
        )
        for side in (0, 1)
    ]
    for side in (0, 1):
        pl.when(sends_to[side])(to_neighbours[side].start)
    for h in range(3, heads):
        start_halo(h)
    for c in range(12):
        fcol[c] = column(factors[c : c + 1, :])

    def normed(x, factor, gain):
        return (x.astype(jnp.float32) * factor * gain).astype(jnp.bfloat16)

    def own_keys(h, carry):
        gains = [g[pl.ds(h, 1), :] for g in (gqv, gkv, gqa, gka)]

        for src, dst, row, g in (
            (qv, qvn, ROW_QV, 0), (kv, kvn, ROW_KV, 1), (qa, qan, ROW_QA, 2), (ka, kan, ROW_KA, 3),
        ):
            for r in range(src.shape[1] // B):
                part = slice(r * B, (r + 1) * B)
                dst[part, :] = normed(src[h, part, :], fcol[row + r], gains[g])
        for kind in (0, 1):
            w = windows[kind, h]
            for t in range(3):
                far = jnp.abs(rows - cols + (t - 1) * B)
                self_bias[h, kind, t * B : (t + 1) * B, :] = jnp.where(far <= w, 0.0, NEG).astype(
                    jnp.float32
                )

        def keep(side, kind, half, m, l, o):
            lanes = slice(half * B, (half + 1) * B)
            row = 4 * side + 2 * kind
            ml[h, row : row + 1, lanes] = m
            ml[h, row + 1 : row + 2, lanes] = l
            os[h, side, kind, :, lanes] = o

        def task(queries, keys, values, windows_of, bias_of, finish):
            lo = min(w[0] for w in windows_of)
            hi = max(w[1] for w in windows_of)
            held = {}

            def scores():
                s = dot_nt(keys[lo:hi, :], queries)
                held["s"] = [
                    s[first - lo : last - lo, i * B : (i + 1) * B]
                    for i, (first, last) in enumerate(windows_of)
                ]

            def weights():
                held["p"] = [softened(held["s"][i] + bias_of(i)) for i in (0, 1)]

            def products():
                p = [
                    padded(held["p"][i][2], windows_of[i][0] - lo, hi - lo) for i in (0, 1)
                ]
                o = dot_nn(values[h, :, lo:hi], jnp.concatenate(p, axis=1))
                finish([(*held["p"][i][:2], o[:, i * B : (i + 1) * B]) for i in (0, 1)])

            return scores, weights, products

        done = {}

        def video_done(pair, kind, results):
            done[pair, kind] = results
            if (pair, 1 - kind) not in done:
                return
            for i in (0, 1):
                b = 2 * pair + i
                if b in (1, 2):
                    o = sum(done[pair, k][i][2] * (1.0 / done[pair, k][i][1]) for k in (0, 1))
                    ov[b * B : (b + 1) * B, columns(h)] = o.astype(jnp.bfloat16).T
                else:
                    for k in (0, 1):
                        keep(pair, k, 0, *done[pair, k][i])

        def audio_done(kind, results):
            for side in (0, 1):
                keep(side, kind, 1, *results[side])

        tasks = []
        for pair in (0, 1):
            q = qvn[2 * pair * B : 2 * (pair + 1) * B, :]
            part = VIDEO_SELF[2 * pair : 2 * pair + 2]

            def self_of(i, pair=pair):
                lo, hi = VIDEO_SELF[2 * pair + i]
                shift = (1 - 2 * pair - i) * B
                return self_bias[h, 0, lo + shift : hi + shift, :]

            tasks.append(
                task(q, kvn, vvt, part, self_of, functools.partial(video_done, pair, 0))
            )
            part = VIDEO_CROSS[2 * pair : 2 * pair + 2]

            def cross_of(i, pair=pair):
                lo, hi = VIDEO_CROSS[2 * pair + i]
                return va_bias[2 * pair + i, 0 : hi - lo, :]

            tasks.append(
                task(q, kan, vat, part, cross_of, functools.partial(video_done, pair, 1))
            )
        tasks.append(
            task(
                qan[...], kvn, vvt, AUDIO_CROSS,
                lambda j: av_bias[j, 0 : AUDIO_CROSS[j][1] - AUDIO_CROSS[j][0], :],
                functools.partial(audio_done, 0),
            )
        )
        tasks.append(
            task(
                qan[...], kan, vat, AUDIO_SELF,
                lambda j: self_bias[h, 1, (1 - j) * B : (3 - j) * B, :],
                functools.partial(audio_done, 1),
            )
        )
        in_turn(tasks)
        for side in (0, 1):
            qe[h, side, :B, :] = qvn[3 * side * B : (3 * side + 1) * B, :]
            qe[h, side, B:, :] = qan[side * B : (side + 1) * B, :]
        return carry

    lax.fori_loop(0, heads, own_keys, 0)

    no_left = jnp.where(me == 0, NEG, 0.0).astype(jnp.float32)
    no_right = jnp.where(me == n_tm - 1, NEG, 0.0).astype(jnp.float32)
    for side in (0, 1):
        pl.when(comes_from[side])(to_neighbours[side].wait_recv)
    for side in (0, 1):
        none = no_left if side == 0 else no_right
        hcol[side, 0] = column(nbr[side, 0:1, :])
        hcol[side, 1] = column(nbr[side, 1:2, :])
        acol = column(nbr[side, 2:3, :])
        vah_bias[side] = near(acol, colsf + (v0 + 3 * side * B)) + none
        avh_bias[side] = near(al[side : side + 1, :], rowsf + (v0 + (-B if side == 0 else 4 * B))) + none

    for side in (0, 1):
        pl.when(sends_to[side])(to_neighbours[side].wait_send)

    def neighbour_keys(h, carry):
        gains = [g[pl.ds(h, 1), :] for g in (gkv, gka)]
        total = {}

        def task(side, kind):
            none = no_left if side == 0 else no_right
            edge = slice(2 * side * B, (2 * side + 1) * B)
            reach = (HALO_AUDIO_CROSS, HALO_VIDEO_CROSS)[kind][side]
            cross = (avh_bias, vah_bias)[kind]
            row = 4 * side + 2 * kind
            held = {}

            def scores():
                keys = normed(halo[h, side, 2 * kind], hcol[side, kind], gains[kind])
                held["s"] = dot_nt(keys, qe[h, side])

            def weights():
                results = []
                for i in (0, 1):
                    lanes = slice(i * B, (i + 1) * B)
                    first, last = (0, B) if i == kind else reach
                    if i == kind:
                        bias = self_bias[h, kind, edge, :] + none
                    else:
                        bias = cross[side, first:last, :]
                    s = held["s"][first:last, lanes] + bias
                    m0 = ml[h, row : row + 1, lanes]
                    m = jnp.maximum(m0, jnp.max(s, axis=0, keepdims=True))
                    e = jnp.exp2((s - m) * C)
                    a = jnp.exp2((m0 - m) * C)
                    l = ml[h, row + 1 : row + 2, lanes] * a + jnp.sum(e, axis=0, keepdims=True)
                    results.append((a, l, padded(e.astype(jnp.bfloat16), first, B)))
                held["p"] = results

            def products():
                values = halo[h, side, 2 * kind + 1].T
                o = dot_nn(values, jnp.concatenate([p[2] for p in held["p"]], axis=1))
                for i in (0, 1):
                    lanes = slice(i * B, (i + 1) * B)
                    a, l, _ = held["p"][i]
                    total[kind, i] = (os[h, side, kind, :, lanes] * a + o[:, lanes]) * (1.0 / l)
                    if kind == 0:
                        os[h, side, kind, :, lanes] = total[kind, i]
                if kind == 1:
                    o = [os[h, side, 0, :, i * B : (i + 1) * B] + total[1, i] for i in (0, 1)]
                    part = slice(3 * side * B, (3 * side + 1) * B)
                    ov[part, columns(h)] = o[0].astype(jnp.bfloat16).T
                    part = slice(side * B, (side + 1) * B)
                    oa[part, columns(h)] = o[1].astype(jnp.bfloat16).T

            return scores, weights, products

        for kind in (0, 1):
            tasks = [task(side, kind) for side in (0, 1)]
            wait_halo(h, 2 * kind)
            for step in (0, 1):
                for steps in tasks:
                    steps[step]()
            wait_halo(h, 2 * kind + 1)
            for steps in tasks:
                steps[2]()
        return carry

    lax.fori_loop(0, heads, neighbour_keys, 0)


def move_kernel(a, b, x, y, sems):
    copies = [
        pltpu.make_async_copy(src, dst, sems.at[i]) for i, (src, dst) in enumerate(((a, x), (b, y)))
    ]
    for copy in copies:
        copy.start()
    for copy in copies:
        copy.wait()


def moved(arrays):
    vmem = pl.BlockSpec(memory_space=pltpu.VMEM)
    hbm = pl.BlockSpec(memory_space=pltpu.HBM)
    return pl.pallas_call(
        move_kernel,
        out_shape=tuple(jax.ShapeDtypeStruct(x.shape, x.dtype) for x in arrays),
        in_specs=[vmem, vmem],
        out_specs=(hbm, hbm),
        scratch_shapes=[pltpu.SemaphoreType.DMA((2,))],
        name="moved",
    )(*[pltpu.with_memory_space_constraint(x, pltpu.VMEM) for x in arrays])


def body(
    q_video, k_video, v_video, q_audio, k_audio, v_audio,
    q_gain_video, k_gain_video, q_gain_audio, k_gain_audio, audio_align, windows,
):
    n_tm = lax.axis_size("tm")
    rows_v, width = q_video.shape
    rows_a = q_audio.shape[0]
    heads = width // HEAD_DIM
    gains = [
        g.reshape(heads, HEAD_DIM) for g in (q_gain_video, k_gain_video, q_gain_audio, k_gain_audio)
    ]
    bf, f32 = jnp.bfloat16, jnp.float32
    vmem = pl.BlockSpec(memory_space=pltpu.VMEM)
    hbm = pl.BlockSpec(memory_space=pltpu.HBM)
    dma = pltpu.SemaphoreType.DMA
    results = pl.pallas_call(
        functools.partial(kernel, n_tm, heads),
        out_shape=(
            pltpu.VMEM(q_video.shape, bf),
            pltpu.VMEM(q_audio.shape, bf),
        ),
        in_specs=[hbm] * 12,
        out_specs=(vmem, vmem),
        scratch_shapes=[
            pltpu.SMEM(windows.shape, jnp.int32),
            *[pltpu.VMEM((heads, B), f32) for _ in range(4)],
            pltpu.VMEM((rows_a // B, B), jnp.int32),
            pltpu.VMEM((heads, rows_v, B), bf),
            pltpu.VMEM((heads, rows_v, B), bf),
            pltpu.VMEM((heads, rows_v, B), bf),
            pltpu.VMEM((heads, rows_a, B), bf),
            pltpu.VMEM((heads, rows_a, B), bf),
            pltpu.VMEM((heads, rows_a, B), bf),
            pltpu.VMEM((heads, 2, 4, B, B), bf),
            pltpu.VMEM((4, 16, B), f32),
            pltpu.VMEM((2, 8, B), f32),
            pltpu.VMEM((2, 8, B), f32),
            pltpu.VMEM((12, B, B), f32),
            pltpu.VMEM((2, 2, B, B), f32),
            pltpu.VMEM((heads, 2, 3 * B, B), f32),
            pltpu.VMEM((4, 160, B), f32),
            pltpu.VMEM((2, 368, B), f32),
            pltpu.VMEM((2, B, B), f32),
            pltpu.VMEM((2, B, B), f32),
            pltpu.VMEM((rows_v, B), bf),
            pltpu.VMEM((rows_v, B), bf),
            pltpu.VMEM((rows_a, B), bf),
            pltpu.VMEM((rows_a, B), bf),
            pltpu.VMEM((heads, B, rows_v), bf),
            pltpu.VMEM((heads, B, rows_a), bf),
            pltpu.VMEM((heads, 2, 2 * B, B), bf),
            pltpu.VMEM((heads, 8, 2 * B), f32),
            pltpu.VMEM((heads, 2, 2, B, 2 * B), f32),
            dma((6,)),
            dma((6, heads)),
            dma((heads, 2, 4)),
            dma((heads, 2, 4)),
            dma((2,)),
            dma((2,)),
            dma((2,)),
            dma((2,)),
        ],
        compiler_params=pltpu.CompilerParams(
            collective_id=0, has_side_effects=True, vmem_limit_bytes=60 * 2**20
        ),
        name="attention",
    )(
        windows, *gains, audio_align.reshape(rows_a // B, B),
        q_video, k_video, v_video, q_audio, k_audio, v_audio,
    )
    return moved(results)


def solution(mesh):
    placed = (P("tm", "head"),) * 6 + (P("head"),) * 4 + (P("tm"), P(None, "head"))
    return jax.shard_map(
        body,
        mesh=mesh,
        in_specs=placed,
        out_specs=(P("tm", "head"), P("tm", "head")),
        check_vma=False,
    )
```
